32 devices in a mesh: dp: 2 (over x), seq: 16 (over z, y, core).
Axes of the slice: x: 2, y: 2, z: 4, core: 2. Of those that a mesh axis runs over, the one named last changes fastest.
Arguments:
- tokens: bfloat16 [2, 4096, 1600], P('dp', 'seq'), may hold values from -6 to 6
- cotangent: bfloat16 [2, 4096, 1600], P('dp', 'seq'), may hold values from -6 to 6
- input_gain: bfloat16 [1600], replicated, may hold values from 0.25 to 1.75
- merged_weight: bfloat16 [1600, 8640], P('seq', 'dp'), may hold values from -0.15625 to 0.15625
- meta_tokens: bfloat16 [1600, 128], P('seq', 'dp'), may hold values from -6 to 6
- select_weight: bfloat16 [3200, 132], P('seq', 'dp'), may hold values from -0.109375 to 0.109375
- step_weight: bfloat16 [3200, 100], P('seq', 'dp'), may hold values from -0.625 to 0.625
- decay_log: bfloat16 [3200, 16], P('seq', 'dp'), may hold values from -7 to 1.5
- conv_weight: bfloat16 [3200, 4], P('seq', 'dp'), may hold values from -3 to 3
- conv_bias: bfloat16 [3200], replicated, may hold values from -3 to 3
- step_bias: bfloat16 [3200], replicated, may hold values from -6 to -1
- skip_gain: bfloat16 [3200], replicated, may hold values from 0.5 to 1.5
- attention_gain: bfloat16 [1600], replicated, may hold values from 0.25 to 1.75
- mamba_gain: bfloat16 [3200], replicated, may hold values from 0.25 to 1.75
- output_weight: bfloat16 [4800, 1600], P('seq', 'dp'), may hold values from -0.1875 to 0.1875
- second_gain: bfloat16 [1600], replicated, may hold values from 0.25 to 1.75
- expand_weight: bfloat16 [1600, 11008], P('seq', 'dp'), may hold values from -0.15625 to 0.15625
- down_weight: bfloat16 [5504, 1600], P('seq', 'dp'), may hold values from -0.078125 to 0.078125
Outputs:
- block_output: bfloat16 [2, 4096, 1600], P('dp', 'seq')
- tokens_grad: float32 [2, 4096, 1600], P('dp', 'seq')
- input_gain_grad: float32 [1600], replicated
- merged_weight_grad: float32 [1600, 8640], P('seq', 'dp')
- meta_tokens_grad: float32 [1600, 128], P('seq', 'dp')
- select_weight_grad: float32 [3200, 132], P('seq', 'dp')
- step_weight_grad: float32 [3200, 100], P('seq', 'dp')
- decay_log_grad: float32 [3200, 16], P('seq', 'dp')
- conv_weight_grad: float32 [3200, 4], P('seq', 'dp')
- conv_bias_grad: float32 [3200], replicated
- step_bias_grad: float32 [3200], replicated
- skip_gain_grad: float32 [3200], replicated
- attention_gain_grad: float32 [1600], replicated
- mamba_gain_grad: float32 [3200], replicated
- output_weight_grad: float32 [4800, 1600], P('seq', 'dp')
- second_gain_grad: float32 [1600], replicated
- expand_weight_grad: float32 [1600, 11008], P('seq', 'dp')
- down_weight_grad: float32 [5504, 1600], P('seq', 'dp')
The draws below stay inside these ranges and needn't reach their ends.
All inputs are finite; a program needn't handle non-finite values.
Results may differ from the reference program's by a relative error of at most 0.015.
Values may be sent and summed in bfloat16 or wider, within the bound.
A program may use at most 576 MiB of HBM per device.

```python
import math
import jax
import jax.numpy as jnp
from jax import lax

D = 1600
HEADS = 25
KVHEADS = 5
HEAD = 64
MINNER = 3200
STATE = 16
DTR = 100
FF = 5504
META = 128
WINDOW = 1024
CONV = 4
QWIDTH = 1600
MERGED = 8640
SEQS = 2
LENGTH = 4096


def steps_of(rng, dims, shards, least, largest):
    def one(dim, blocks):
        heights = jax.random.uniform(jax.random.fold_in(jax.random.fold_in(rng, 6), dim), (blocks,), jnp.float32, least / len(shards), largest / len(shards))
        return jnp.repeat(jnp.exp(heights), dims[dim] // blocks).reshape((-1,) + (1,) * (len(dims) - dim - 1))

    level = one(*shards[0])
    for cut in shards[1:]:
        level = level * one(*cut)
    return level


def normal_values(rng, shape, spread, reach, split=(), held_as=jnp.bfloat16):
    drawn = spread * jax.random.normal(rng, shape, jnp.float32)
    if split:
        drawn = drawn * steps_of(rng, shape, split, -0.22, 0.18)
    return jnp.clip(drawn, -reach, reach).astype(held_as)


def setup_inputs(seed: int = 0) -> dict:
    streams_of = jax.random.split(jax.random.key(seed), 19)
    return {
        "tokens": normal_values(streams_of[0], (SEQS, LENGTH, D), 1.0, 6.0, ((0, 2), (1, 16))),
        "cotangent": normal_values(streams_of[1], (SEQS, LENGTH, D), 1.0, 6.0, ((0, 2), (1, 16))),
        "input_gain": jnp.clip(1.0 + 0.15 * jax.random.normal(streams_of[2], (D,), jnp.float32), 0.25, 1.75).astype(jnp.bfloat16),
        "merged_weight": normal_values(streams_of[3], (D, MERGED), D ** -0.5, 0.15625, ((0, 16), (1, 2))),
        "meta_tokens": normal_values(streams_of[4], (D, META), 1.0, 6.0, ((0, 16), (1, 2))),
        "select_weight": normal_values(streams_of[5], (MINNER, DTR + 2 * STATE), MINNER ** -0.5, 0.109375, ((0, 16), (1, 2))),
        "step_weight": normal_values(streams_of[6], (MINNER, DTR), DTR ** -0.5, 0.625, ((0, 16), (1, 2))),
        "decay_log": jnp.clip(-7.0 + 8.5 * jax.random.uniform(streams_of[7], (MINNER, STATE), jnp.float32) ** steps_of(streams_of[7], (MINNER, STATE), ((0, 16), (1, 2)), -0.2, 0.2), -7.0, 1.5).astype(jnp.bfloat16),
        "conv_weight": normal_values(streams_of[8], (MINNER, CONV), CONV ** -0.5, 3.0, ((0, 16), (1, 2))),
        "conv_bias": normal_values(streams_of[9], (MINNER,), 0.5, 3.0),
        "step_bias": jnp.clip(jax.random.uniform(streams_of[10], (MINNER,), jnp.float32, -6.0, -1.0), -6.0, -1.0).astype(jnp.bfloat16),
        "skip_gain": jnp.clip(jax.random.uniform(streams_of[11], (MINNER,), jnp.float32, 0.5, 1.5), 0.5, 1.5).astype(jnp.bfloat16),
        "attention_gain": jnp.clip(1.0 + 0.15 * jax.random.normal(streams_of[12], (QWIDTH,), jnp.float32), 0.25, 1.75).astype(jnp.bfloat16),
        "mamba_gain": jnp.clip(1.0 + 0.15 * jax.random.normal(streams_of[13], (MINNER,), jnp.float32), 0.25, 1.75).astype(jnp.bfloat16),
        "output_weight": normal_values(streams_of[14], (QWIDTH + MINNER, D), ((QWIDTH + MINNER) // 4) ** -0.5, 0.1875, ((0, 16), (1, 2))),
        "second_gain": jnp.clip(1.0 + 0.15 * jax.random.normal(streams_of[15], (D,), jnp.float32), 0.25, 1.75).astype(jnp.bfloat16),
        "expand_weight": normal_values(streams_of[16], (D, 2 * FF), D ** -0.5, 0.15625, ((0, 16), (1, 2))),
        "down_weight": normal_values(streams_of[17], (FF, D), FF ** -0.5, 0.078125, ((0, 16), (1, 2))),
    }


highest = lax.Precision.HIGHEST
epsilon = 1e-06

@jax.custom_vjp
def low(v):
    return lax.optimization_barrier(v.astype(jnp.bfloat16)).astype(jnp.float32)

@jax.custom_vjp
def low_back(v):
    return v

def low_keep(v):
    return (low(v), None)

def low_pass(kept, grad):
    return (grad,)

def back_keep(v):
    return (v, None)

def back_low(kept, grad):
    return (low(grad),)
low.defvjp(low_keep, low_pass)
low_back.defvjp(back_keep, back_low)

def matmul(left_side, right_side):
    return jnp.dot(left_side, right_side, precision=highest)

def rms_norm(values, gain_row):
    return values * lax.rsqrt(lax.optimization_barrier(jnp.mean(values * values, axis=-1, keepdims=True)) + epsilon) * gain_row

def silu_gate(values):
    return values * jax.nn.sigmoid(values)

def softplus(values):
    return jnp.log1p(jnp.exp(values))

def attend(queries, key_rows, value_rows, meta_keys, meta_values):
    length = queries.shape[0]
    block_len = math.gcd(512, length)
    group_size = HEADS // KVHEADS
    score_scale = HEAD ** (-0.5)
    padding = jnp.zeros((WINDOW, KVHEADS * HEAD), jnp.float32)
    key_pad = jnp.concatenate([padding, key_rows], axis=0)
    value_pad = jnp.concatenate([padding, value_rows], axis=0)
    meta_key_heads = meta_keys.reshape(META, KVHEADS, HEAD)
    meta_value_heads = meta_values.reshape(META, KVHEADS, HEAD)

    def one_block(anchor):
        row_block = lax.dynamic_slice_in_dim(queries, anchor, block_len, 0).reshape(block_len, KVHEADS, group_size, HEAD)
        key_block = lax.dynamic_slice_in_dim(key_pad, anchor, WINDOW + block_len, 0).reshape(WINDOW + block_len, KVHEADS, HEAD)
        value_block = lax.dynamic_slice_in_dim(value_pad, anchor, WINDOW + block_len, 0).reshape(WINDOW + block_len, KVHEADS, HEAD)
        target = anchor + jnp.arange(block_len, dtype=jnp.int32)
        source = anchor - WINDOW + jnp.arange(WINDOW + block_len, dtype=jnp.int32)
        distance = target[:, None] - source[None, :]
        visible = (distance >= 0) & (distance < WINDOW) & (source[None, :] >= 0)
        nearby = low_back(jnp.einsum('qkgd,lkd->kgql', row_block, key_block, precision=highest) * score_scale)
        distant = low_back(jnp.einsum('qkgd,mkd->kgqm', row_block, meta_key_heads, precision=highest) * score_scale)
        nearby = jnp.where(visible, nearby, -1e+30)
        scores = jnp.concatenate([distant, nearby], axis=-1)
        row_max = lax.optimization_barrier(jnp.max(scores, axis=-1, keepdims=True))
        powers = jnp.exp(scores - row_max)
        weights = low(powers / lax.optimization_barrier(jnp.sum(powers, axis=-1, keepdims=True)))
        result = jnp.einsum('kgqm,mkd->qkgd', weights[..., :META], meta_value_heads, precision=highest)
        result = result + jnp.einsum('kgql,lkd->qkgd', weights[..., META:], value_block, precision=highest)
        return result.reshape(block_len, HEADS * HEAD)
    anchors = jnp.arange(length // block_len, dtype=jnp.int32) * block_len
    return lax.map(jax.checkpoint(one_block), anchors).reshape(length, HEADS * HEAD)

def selective(signal, step_size, write_mix, read_mix, decays, skip_gain):
    length = signal.shape[0]
    block_len = math.gcd(128, length)

    def one_step(states, inputs):
        value_row, step_row, write_row, read_row = inputs
        states = jnp.exp(step_row[None, :] * decays) * states + (step_row * value_row)[None, :] * write_row[:, None]
        return (states, lax.optimization_barrier(jnp.sum(read_row[:, None] * states, axis=0)))

    def run_block(states, inputs):
        return lax.scan(one_step, states, inputs)
    pieces = tuple((member.reshape(length // block_len, block_len, member.shape[1]) for member in (signal, step_size, write_mix, read_mix)))
    initial = jnp.zeros((STATE, MINNER), jnp.float32)
    outputs = lax.scan(jax.checkpoint(run_block), initial, pieces)[1]
    return outputs.reshape(length, MINNER) + skip_gain * signal

def forward(tokens, input_gain, merged_weight, meta_tokens, select_weight, step_weight, decay_log, conv_weight, conv_bias, step_bias, skip_gain, attention_gain, mamba_gain, output_weight, second_gain, expand_weight, down_weight):
    query_width = HEADS * HEAD
    key_width = KVHEADS * HEAD
    inner_start = query_width + 2 * key_width
    meta_normed = low(rms_norm(meta_tokens.T, input_gain))
    meta_pairs = low(matmul(meta_normed, merged_weight[:, query_width:inner_start]))
    decays = -jnp.exp(decay_log.T)

    def one_sequence(sequence):
        length = sequence.shape[0]
        normed = low(rms_norm(sequence, input_gain))
        projected = matmul(normed, merged_weight)
        queries = low_back(low(projected[:, :query_width]))
        key_rows = low_back(low(projected[:, query_width:query_width + key_width]))
        value_rows = low_back(low(projected[:, query_width + key_width:inner_start]))
        inner_path = low_back(low(projected[:, inner_start:inner_start + MINNER]))
        gate_path = low_back(projected[:, inner_start + MINNER:])
        attended = low_back(attend(queries, key_rows, value_rows, meta_pairs[:, :key_width], meta_pairs[:, key_width:]))
        padded = jnp.concatenate([jnp.zeros((CONV - 1, MINNER), jnp.float32), inner_path], axis=0)
        convolved = conv_bias
        for offset in range(CONV):
            convolved = convolved + conv_weight[:, offset] * padded[offset:offset + length]
        signal = low(silu_gate(convolved))
        selected = low_back(matmul(signal, select_weight))
        step_raw = low(selected[:, :DTR])
        step_size = softplus(low_back(matmul(step_raw, step_weight.T)) + step_bias)
        scanned = selective(signal, step_size, selected[:, DTR:DTR + STATE], selected[:, DTR + STATE:], decays, skip_gain)
        mamba_path = scanned * silu_gate(gate_path)
        joined = low(jnp.concatenate([rms_norm(attended, attention_gain), rms_norm(mamba_path, mamba_gain)], axis=1))
        hidden = sequence + low_back(0.5 * matmul(joined, output_weight))
        normed_two = low(rms_norm(hidden, second_gain))
        expanded = matmul(normed_two, expand_weight)
        gate_pre = low_back(expanded[:, :FF])
        up_pre = low_back(expanded[:, FF:])
        active = low(silu_gate(gate_pre) * up_pre)
        return hidden + low_back(matmul(active, down_weight))
    return lax.map(one_sequence, tokens)

def reference(tokens, cotangent, input_gain, merged_weight, meta_tokens, select_weight, step_weight, decay_log, conv_weight, conv_bias, step_bias, skip_gain, attention_gain, mamba_gain, output_weight, second_gain, expand_weight, down_weight):
    result, pullback = jax.vjp(forward, tokens.astype(jnp.float32), input_gain.astype(jnp.float32), merged_weight.astype(jnp.float32), meta_tokens.astype(jnp.float32), select_weight.astype(jnp.float32), step_weight.astype(jnp.float32), decay_log.astype(jnp.float32), conv_weight.astype(jnp.float32), conv_bias.astype(jnp.float32), step_bias.astype(jnp.float32), skip_gain.astype(jnp.float32), attention_gain.astype(jnp.float32), mamba_gain.astype(jnp.float32), output_weight.astype(jnp.float32), second_gain.astype(jnp.float32), expand_weight.astype(jnp.float32), down_weight.astype(jnp.float32))
    gradients = pullback(cotangent.astype(jnp.float32))
    return (result.astype(jnp.bfloat16), gradients[0], gradients[1], gradients[2], gradients[3], gradients[4], gradients[5], gradients[6], gradients[7], gradients[8], gradients[9], gradients[10], gradients[11], gradients[12], gradients[13], gradients[14], gradients[15], gradients[16])
```

```python
import functools

import jax
import jax.numpy as jnp
from jax import lax
from jax.experimental import pallas as pl
from jax.experimental.pallas import tpu as pltpu
from jax.sharding import Mesh
from jax.sharding import PartitionSpec as P

HEADS = 25
KVHEADS = 5
HEAD = 64
MINNER = 3200
STATE = 16
DTR = 100
META = 128
WINDOW = 1024
CONV = 4
epsilon = 1e-06
LANES = 128
STEPS = 8
LOG2E = 1.4426950408889634
VMEM_LIMIT = 60 * 1024 * 1024


def lane_tiles(width):
    return [slice(at, min(at + LANES, width)) for at in range(0, width, LANES)]


def chunk_of(channels):
    for tiles in (5, 4, 6, 3, 2, 7, 1):
        if channels % (tiles * LANES) == 0:
            return tiles * LANES
    return channels


def fold(rows):
    sub = lax.broadcasted_iota(jnp.int32, rows[0].shape, 0)
    for bit in (1, 2, 4):
        clear = (sub & bit) == 0
        rows = [
            jnp.where(clear, one, two) + pltpu.roll(jnp.where(clear, two, one), bit, 0)
            for one, two in zip(rows[0::2], rows[1::2])
        ]
    return rows[0]


def halves(product):
    return product[:8] + product[8:]


def ends_kernel(step_ref, signal_ref, write_ref, decay_ref, end_ref):
    length, width = step_ref.shape
    tiles = lane_tiles(width)
    rates = [decay_ref[:, tile] * LOG2E for tile in tiles]

    def block(at, states):
        states = list(states)
        rows = pl.ds(pl.multiple_of(at * STEPS, STEPS), STEPS)
        step = step_ref[rows, :]
        drive = step * signal_ref[rows, :].astype(jnp.float32)
        for i in range(STEPS):
            write = write_ref[at * STEPS + i]
            for j, tile in enumerate(tiles):
                factor = jnp.exp2(step[i : i + 1, tile] * rates[j])
                states[j] = factor * states[j] + drive[i : i + 1, tile] * write[:, : tile.stop - tile.start]
        return tuple(states)

    zero = tuple(jnp.zeros((STATE, tile.stop - tile.start), jnp.float32) for tile in tiles)
    final = lax.fori_loop(0, length // STEPS, block, zero)
    for j, tile in enumerate(tiles):
        end_ref[:, tile] = final[j]


def pull_kernel(step_ref, grad_ref, read_ref, decay_ref, end_ref):
    length, width = step_ref.shape
    tiles = lane_tiles(width)
    rates = [decay_ref[:, tile] * LOG2E for tile in tiles]
    blocks = length // STEPS

    def block(k, states):
        at = blocks - 1 - k
        states = list(states)
        rows = pl.ds(pl.multiple_of(at * STEPS, STEPS), STEPS)
        step = step_ref[rows, :]
        grad = grad_ref[rows, :]
        for i in reversed(range(STEPS)):
            read = read_ref[at * STEPS + i]
            for j, tile in enumerate(tiles):
                factor = jnp.exp2(step[i : i + 1, tile] * rates[j])
                states[j] = factor * (states[j] + grad[i : i + 1, tile] * read[:, : tile.stop - tile.start])
        return tuple(states)

    zero = tuple(jnp.zeros((STATE, tile.stop - tile.start), jnp.float32) for tile in tiles)
    final = lax.fori_loop(0, blocks, block, zero)
    for j, tile in enumerate(tiles):
        end_ref[:, tile] = final[j]


def carry_over(position, count, reverse, rates, totals_ref, ends_ref, tile):
    def step(k, state):
        at = count - 1 - k if reverse else k
        reached = at > position if reverse else at < position
        factor = jnp.exp2(totals_ref[at, :, tile] * rates)
        new = factor * state + ends_ref[at, :, tile].astype(jnp.float32)
        return jnp.where(reached, new, state)

    return lax.fori_loop(0, count, step, jnp.zeros(rates.shape, jnp.float32))


def scan_kernel(
    position_ref, step_ref, signal_ref, write_ref, read_ref, decay_ref, skip_ref,
    totals_ref, ends_ref, out_ref, enter_ref,
):
    length, width = step_ref.shape
    tiles = lane_tiles(width)
    rates = [decay_ref[:, tile] * LOG2E for tile in tiles]
    enter = tuple(
        carry_over(position_ref[0], totals_ref.shape[0], False, rates[j], totals_ref, ends_ref, tile)
        for j, tile in enumerate(tiles)
    )
    for j, tile in enumerate(tiles):
        enter_ref[:, tile] = enter[j]

    def block(at, states):
        states = list(states)
        rows = pl.ds(pl.multiple_of(at * STEPS, STEPS), STEPS)
        step = step_ref[rows, :]
        signal = signal_ref[rows, :].astype(jnp.float32)
        drive = step * signal
        parts = [[] for tile in tiles]
        for i in range(STEPS):
            write = write_ref[at * STEPS + i]
            read = read_ref[at * STEPS + i]
            for j, tile in enumerate(tiles):
                wide = tile.stop - tile.start
                factor = jnp.exp2(step[i : i + 1, tile] * rates[j])
                states[j] = factor * states[j] + drive[i : i + 1, tile] * write[:, :wide]
                parts[j].append(halves(read[:, :wide] * states[j]))
        for j, tile in enumerate(tiles):
            out_ref[rows, tile] = fold(parts[j]) + skip_ref[:, tile] * signal[:, tile]
        return tuple(states)

    lax.fori_loop(0, length // STEPS, block, enter)


def scan_back_kernel(
    position_ref, step_ref, signal_ref, grad_ref, write_ref, read_ref, decay_ref, skip_ref,
    enter_ref, totals_ref, pulls_ref,
    signal_grad_ref, step_grad_ref, write_grad_ref, read_grad_ref, decay_grad_ref, skip_grad_ref,
    states_ref, factors_ref,
):
    length, width = step_ref.shape
    tiles = lane_tiles(width)
    blocks = length // STEPS
    decays = [decay_ref[:, tile] for tile in tiles]

    @pl.when(pl.program_id(0) == 0)
    def _():
        write_grad_ref[...] = jnp.zeros_like(write_grad_ref)
        read_grad_ref[...] = jnp.zeros_like(read_grad_ref)

    rates = [decay * LOG2E for decay in decays]
    states_ref[0] = enter_ref[...]

    def forward(at, states):
        states = list(states)
        rows = pl.ds(pl.multiple_of(at * STEPS, STEPS), STEPS)
        step = step_ref[rows, :]
        drive = step * signal_ref[rows, :].astype(jnp.float32)
        for i in range(STEPS):
            write = write_ref[at * STEPS + i]
            for j, tile in enumerate(tiles):
                factor = jnp.exp2(step[i : i + 1, tile] * rates[j])
                states[j] = factor * states[j] + drive[i : i + 1, tile] * write[:, : tile.stop - tile.start]
                factors_ref[at * STEPS + i, :, tile] = factor
                states_ref[at * STEPS + i + 1, :, tile] = states[j]
        return tuple(states)

    lax.fori_loop(0, blocks, forward, tuple(enter_ref[:, tile] for tile in tiles))

    leaving = tuple(
        carry_over(position_ref[0], totals_ref.shape[0], True, rates[j], totals_ref, pulls_ref, tile)
        for j, tile in enumerate(tiles)
    )
    zero = tuple(jnp.zeros_like(decay) for decay in decays)
    zero_row = tuple(jnp.zeros((STEPS, tile.stop - tile.start), jnp.float32) for tile in tiles)

    def backward(k, carry):
        at = blocks - 1 - k
        adjoint, decay_sum, skip_sum = (list(part) for part in carry)
        rows = pl.ds(pl.multiple_of(at * STEPS, STEPS), STEPS)
        step = step_ref[rows, :]
        signal = signal_ref[rows, :].astype(jnp.float32)
        grad = grad_ref[rows, :]
        drive = step * signal
        by_write = [[None] * STEPS for tile in tiles]
        by_decay = [[None] * STEPS for tile in tiles]
        for i in reversed(range(STEPS)):
            write = write_ref[at * STEPS + i]
            read = read_ref[at * STEPS + i]
            write_sum = None
            read_sum = None
            for j, tile in enumerate(tiles):
                wide = tile.stop - tile.start
                row = grad[i : i + 1, tile]
                whole = adjoint[j] + read[:, :wide] * row
                adjoint[j] = factors_ref[at * STEPS + i, :, tile] * whole
                kept = adjoint[j] * states_ref[at * STEPS + i, :, tile]
                decay_sum[j] = decay_sum[j] + step[i : i + 1, tile] * kept
                by_decay[j][i] = halves(decays[j] * kept)
                by_write[j][i] = halves(write[:, :wide] * whole)
                write_part = drive[i : i + 1, tile] * whole
                read_part = row * states_ref[at * STEPS + i + 1, :, tile]
                write_sum = write_part if write_sum is None else write_sum + write_part
                read_sum = read_part if read_sum is None else read_sum + read_part
            write_grad_ref[at * STEPS + i] += write_sum
            read_grad_ref[at * STEPS + i] += read_sum
        for j, tile in enumerate(tiles):
            written = fold(by_write[j])
            signal_grad_ref[rows, tile] = step[:, tile] * written + skip_ref[:, tile] * grad[:, tile]
            step_grad_ref[rows, tile] = signal[:, tile] * written + fold(by_decay[j])
            skip_sum[j] = skip_sum[j] + grad[:, tile] * signal[:, tile]
        return tuple(adjoint), tuple(decay_sum), tuple(skip_sum)

    carry = lax.fori_loop(0, blocks, backward, (leaving, zero, zero_row))
    for j, tile in enumerate(tiles):
        decay_grad_ref[:, tile] = carry[1][j]
        skip_grad_ref[:, tile] = carry[2][j]


def by_chunk(rows, chunk):
    return pl.BlockSpec((rows, chunk), lambda c: (0, c))


def stacked(count, rows, chunk):
    return pl.BlockSpec((count, rows, chunk), lambda c: (0, 0, c))


def whole(shape):
    return pl.BlockSpec(shape, lambda c: (0,) * len(shape))


def params():
    return pltpu.CompilerParams(vmem_limit_bytes=VMEM_LIMIT, dimension_semantics=("arbitrary",))


def scan_ends(step_size, signal, write_wide, decays):
    length, channels = step_size.shape
    chunk = chunk_of(channels)
    return pl.pallas_call(
        ends_kernel,
        grid=(channels // chunk,),
        in_specs=[by_chunk(length, chunk), by_chunk(length, chunk), whole(write_wide.shape), by_chunk(STATE, chunk)],
        out_specs=by_chunk(STATE, chunk),
        out_shape=jax.ShapeDtypeStruct((STATE, channels), jnp.float32),
        compiler_params=params(),
        name="scan_ends",
    )(step_size, signal, write_wide, decays)


def scan_pulls(step_size, grad, read_wide, decays):
    length, channels = step_size.shape
    chunk = chunk_of(channels)
    return pl.pallas_call(
        pull_kernel,
        grid=(channels // chunk,),
        in_specs=[by_chunk(length, chunk), by_chunk(length, chunk), whole(read_wide.shape), by_chunk(STATE, chunk)],
        out_specs=by_chunk(STATE, chunk),
        out_shape=jax.ShapeDtypeStruct((STATE, channels), jnp.float32),
        compiler_params=params(),
        name="scan_pulls",
    )(step_size, grad, read_wide, decays)


def scan_forward(position, step_size, signal, write_wide, read_wide, decays, skip, totals, ends):
    length, channels = step_size.shape
    chunk = chunk_of(channels)
    parts = totals.shape[0]
    return pl.pallas_call(
        scan_kernel,
        grid=(channels // chunk,),
        in_specs=[
            pl.BlockSpec(memory_space=pltpu.SMEM),
            by_chunk(length, chunk), by_chunk(length, chunk), whole(write_wide.shape), whole(read_wide.shape),
            by_chunk(STATE, chunk), by_chunk(1, chunk), stacked(parts, 1, chunk), stacked(parts, STATE, chunk),
        ],
        out_specs=[by_chunk(length, chunk), by_chunk(STATE, chunk)],
        out_shape=[
            jax.ShapeDtypeStruct((length, channels), jnp.float32),
            jax.ShapeDtypeStruct((STATE, channels), jnp.float32),
        ],
        compiler_params=params(),
        name="scan_forward",
    )(position, step_size, signal, write_wide, read_wide, decays, skip, totals, ends)


def scan_backward(position, step_size, signal, grad, write_wide, read_wide, decays, skip, enter, totals, pulls):
    length, channels = step_size.shape
    chunk = chunk_of(channels)
    parts = totals.shape[0]
    return pl.pallas_call(
        scan_back_kernel,
        grid=(channels // chunk,),
        in_specs=[
            pl.BlockSpec(memory_space=pltpu.SMEM),
            by_chunk(length, chunk), by_chunk(length, chunk), by_chunk(length, chunk),
            whole(write_wide.shape), whole(read_wide.shape),
            by_chunk(STATE, chunk), by_chunk(1, chunk), by_chunk(STATE, chunk), stacked(parts, 1, chunk),
            stacked(parts, STATE, chunk),
        ],
        out_specs=[
            by_chunk(length, chunk), by_chunk(length, chunk), whole(write_wide.shape), whole(read_wide.shape),
            by_chunk(STATE, chunk), by_chunk(STEPS, chunk),
        ],
        out_shape=[
            jax.ShapeDtypeStruct((length, channels), jnp.float32),
            jax.ShapeDtypeStruct((length, channels), jnp.float32),
            jax.ShapeDtypeStruct(write_wide.shape, jnp.float32),
            jax.ShapeDtypeStruct(read_wide.shape, jnp.float32),
            jax.ShapeDtypeStruct((STATE, channels), jnp.float32),
            jax.ShapeDtypeStruct((STEPS, channels), jnp.float32),
        ],
        scratch_shapes=[
            pltpu.VMEM((length + 1, STATE, chunk), jnp.float32),
            pltpu.VMEM((length, STATE, chunk), jnp.float32),
        ],
        compiler_params=params(),
        name="scan_backward",
    )(position, step_size, signal, grad, write_wide, read_wide, decays, skip, enter, totals, pulls)


def key_blocks(keys, span, count):
    meta = keys - count * span
    return [(0, meta, None)] + [(meta + b * span, span, b) for b in range(count)]


def masked(scores, place, count, position, other):
    if place is None:
        return scores
    row = lax.broadcasted_iota(jnp.int32, scores.shape, 0)
    column = lax.broadcasted_iota(jnp.int32, scores.shape, 1)
    if place == count - 1:
        return jnp.where(row <= column, scores, other)
    there = position + place >= count - 1
    if place == 0:
        return jnp.where((row > column) & there, scores, other)
    return jnp.where(there, scores, other)


def attend_kernel(count, position_ref, query_ref, key_ref, value_ref, out_ref, log_ref):
    position = position_ref[0]
    span = query_ref.shape[1]
    group = query_ref.shape[0] // HEAD
    blocks = key_blocks(key_ref.shape[1], span, count)
    for head in range(group):
        rows = slice(head * HEAD, (head + 1) * HEAD)
        query = query_ref[rows, :] * (HEAD**-0.5)
        scores = [
            masked(
                jnp.dot(key_ref[0, at : at + size, :], query, preferred_element_type=jnp.float32),
                place, count, position, -1e30,
            )
            for at, size, place in blocks
        ]
        top = functools.reduce(jnp.maximum, [jnp.max(part, axis=0, keepdims=True) for part in scores])
        powers = [jnp.exp(part - top) for part in scores]
        total = sum(jnp.sum(part, axis=0, keepdims=True) for part in powers)
        out = sum(
            jnp.dot(value_ref[:, at : at + size], part.astype(jnp.bfloat16), preferred_element_type=jnp.float32)
            for (at, size, place), part in zip(blocks, powers)
        )
        out_ref[rows, :] = out / total
        log_ref[0, head : head + 1, :] = top + jnp.log(total)


def attend_back_kernel(
    count, position_ref, query_ref, grad_ref, out_ref, log_ref, key_ref, value_ref, key_turned_ref,
    query_grad_ref, key_grad_ref, value_grad_ref,
):
    position = position_ref[0]
    span = query_ref.shape[1]
    group = query_ref.shape[0] // HEAD
    blocks = key_blocks(key_ref.shape[1], span, count)
    turned = (((1,), (1,)), ((), ()))
    for head in range(group):
        rows = slice(head * HEAD, (head + 1) * HEAD)
        query = query_ref[rows, :] * (HEAD**-0.5)
        grad = grad_ref[rows, :]
        along = jnp.sum(grad.astype(jnp.float32) * out_ref[rows, :], axis=0, keepdims=True)
        log_total = log_ref[0, head : head + 1, :]
        query_sum = jnp.zeros((HEAD, span), jnp.float32)
        for at, size, place in blocks:
            keys = slice(at, at + size)
            score = jnp.dot(key_ref[0, keys, :], query, preferred_element_type=jnp.float32)
            prob = jnp.exp(masked(score, place, count, position, -1e30) - log_total)
            prob_grad = jnp.dot(value_ref[0, keys, :], grad, preferred_element_type=jnp.float32)
            score_grad = (prob * (prob_grad - along)).astype(jnp.bfloat16)
            query_sum += jnp.dot(key_turned_ref[:, keys], score_grad, preferred_element_type=jnp.float32)
            by_key = lax.dot_general(score_grad, query, turned, preferred_element_type=jnp.float32)
            by_value = lax.dot_general(prob.astype(jnp.bfloat16), grad, turned, preferred_element_type=jnp.float32)
            if head == 0:
                key_grad_ref[0, keys, :] = by_key
                value_grad_ref[0, keys, :] = by_value
            else:
                key_grad_ref[0, keys, :] += by_key
                value_grad_ref[0, keys, :] += by_value
        query_grad_ref[rows, :] = (query_sum * (HEAD**-0.5)).astype(query_grad_ref.dtype)


def by_head(rows, columns):
    return pl.BlockSpec((rows, columns), lambda g: (g, 0))


def head_stack(rows, columns):
    return pl.BlockSpec((1, rows, columns), lambda g: (g, 0, 0))


def attend(position, query_turned, keys, value_turned, count):
    span = query_turned.shape[1]
    group = query_turned.shape[0] // KVHEADS
    total = keys.shape[1]
    return pl.pallas_call(
        functools.partial(attend_kernel, count),
        grid=(KVHEADS,),
        in_specs=[
            pl.BlockSpec(memory_space=pltpu.SMEM),
            by_head(group, span), head_stack(total, HEAD), by_head(HEAD, total),
        ],
        out_specs=[by_head(group, span), head_stack(8, span)],
        out_shape=[
            jax.ShapeDtypeStruct(query_turned.shape, jnp.float32),
            jax.ShapeDtypeStruct((KVHEADS, 8, span), jnp.float32),
        ],
        compiler_params=params(),
        name="attend",
    )(position, query_turned, keys, value_turned)


def attend_back(position, query_turned, grad_turned, out_turned, logs, keys, values, key_turned, count):
    span = query_turned.shape[1]
    group = query_turned.shape[0] // KVHEADS
    total = keys.shape[1]
    return pl.pallas_call(
        functools.partial(attend_back_kernel, count),
        grid=(KVHEADS,),
        in_specs=[
            pl.BlockSpec(memory_space=pltpu.SMEM),
            by_head(group, span), by_head(group, span), by_head(group, span), head_stack(8, span),
            head_stack(total, HEAD), head_stack(total, HEAD), by_head(HEAD, total),
        ],
        out_specs=[by_head(group, span), head_stack(total, HEAD), head_stack(total, HEAD)],
        out_shape=[
            jax.ShapeDtypeStruct(query_turned.shape, jnp.bfloat16),
            jax.ShapeDtypeStruct(keys.shape, jnp.float32),
            jax.ShapeDtypeStruct(keys.shape, jnp.float32),
        ],
        compiler_params=params(),
        name="attend_back",
    )(position, query_turned, grad_turned, out_turned, logs, keys, values, key_turned)


SEQ = ("chip", "core")
ALL = ("dp",) + SEQ


def from_behind(array, by):
    size = lax.axis_size("chip") * lax.axis_size("core")
    pairs = [(i, i + by) for i in range(size) if 0 <= i + by < size]
    return lax.ppermute(array, SEQ, pairs)


def swap(array, axis="dp"):
    return lax.ppermute(array, axis, [(0, 1), (1, 0)])


def sum_everywhere(array):
    array = array + swap(array, "core")
    chips = lax.axis_size("chip")
    step = 1
    while step < chips:
        array = array + lax.ppermute(array, "chip", [(i, i ^ step) for i in range(chips)])
        step *= 2
    return array + swap(array)


def parity_kernel(parts, block, core_ref, in_ref, own_ref, other_ref):
    values = in_ref[...].astype(jnp.float32)
    even, odd = [
        jnp.concatenate(
            [values[:, at * block : (at + 1) * block] for at in range(core, parts, 2)], axis=1
        )
        for core in (0, 1)
    ]
    own = core_ref[0] == 0
    own_ref[...] = jnp.where(own, even, odd).astype(own_ref.dtype)
    other_ref[...] = jnp.where(own, odd, even).astype(other_ref.dtype)


def parity_columns(array, parts, block):
    rows = array.shape[0]
    step = 64 if rows % 64 == 0 else rows
    half = pl.BlockSpec((step, parts // 2 * block), lambda r: (r, 0))
    return pl.pallas_call(
        functools.partial(parity_kernel, parts, block),
        grid=(rows // step,),
        in_specs=[
            pl.BlockSpec(memory_space=pltpu.SMEM),
            pl.BlockSpec((step, parts * block), lambda r: (r, 0)),
        ],
        out_specs=[half, half],
        out_shape=[jax.ShapeDtypeStruct((rows, parts // 2 * block), array.dtype)] * 2,
        compiler_params=params(),
        name="parity_columns",
    )(jnp.reshape(lax.axis_index("core"), (1,)).astype(jnp.int32), array)


def grad_parts(left, right, scale=1.0):
    kept, given = left
    sent = (scale * dot_rows(given, right)).astype(jnp.bfloat16)
    got = swap(sent, "core")
    return (scale * dot_rows(kept, right) + got.astype(jnp.float32)).astype(jnp.bfloat16)


def scatter_rows(total, rows):
    chips = lax.axis_size("chip")
    return lax.psum_scatter(total.reshape(chips, rows, -1), "chip", scatter_dimension=0)


def rms_norm(values, gain_row, count):
    mean = jnp.sum(values * values, axis=-1, keepdims=True) * (1.0 / count)
    return values * lax.rsqrt(mean + epsilon) * gain_row


def silu_gate(values):
    return values * jax.nn.sigmoid(values)


def softplus(values):
    return jnp.log1p(jnp.exp(values))


def ceil8(rows):
    return -(-rows // 8) * 8


def pad_rows(array, rows):
    return jnp.pad(array, ((0, rows - array.shape[0]), (0, 0)))


MESH = pl.DeviceIdType.MESH


def chip_at(place, chips):
    place = place % chips
    late = place // (chips // 2)
    return (1 - late) * 2 * place + late * (2 * (chips - 1 - place) + 1)


def place_of(chip, chips):
    odd = chip % 2
    return (1 - odd) * (chip // 2) + odd * (chips - 1 - chip // 2)


def gather_kernel(cuts, others, *refs):
    count = len(cuts)
    whole = count + others
    ins, singles = refs[:count], refs[count:whole]
    outs, singles_out = refs[whole : whole + count], refs[whole + count : 2 * whole]
    local_sem, send_sem, recv_sem = refs[2 * whole :]
    dp, chip, core = (lax.axis_index(name) for name in ALL)
    chips = lax.axis_size("chip")
    place = place_of(chip, chips)
    ahead, behind = chip_at(place + 1, chips), chip_at(place + chips - 1, chips)
    to_ahead, to_behind = (dp, ahead, core), (dp, behind, core)
    across, beside = (1 - dp, chip, core), (dp, chip, 1 - core)
    sent = []

    def start(source, target, device):
        index = len(sent)
        copy = pltpu.make_async_remote_copy(
            src_ref=source,
            dst_ref=target,
            send_sem=send_sem.at[index],
            recv_sem=recv_sem.at[index],
            device_id=device,
            device_id_type=MESH,
        )
        copy.start()
        sent.append(copy)
        return copy

    kept = [
        pltpu.make_async_copy(ins[t], outs[t].at[dp, chip, core], local_sem.at[t])
        for t in range(count)
    ]
    for copy in kept:
        copy.start()

    barrier = pltpu.get_barrier_semaphore()
    for device in (to_ahead, to_behind, across, beside):
        pl.semaphore_signal(barrier, inc=1, device_id=device, device_id_type=MESH)
    pl.semaphore_wait(barrier, 4)

    def early(t, at):
        return outs[t].at[:, chip_at(at, chips), core, :, pl.ds(0, cuts[t])]

    def late(t, side, at):
        wide = outs[t].shape[-1] - cuts[t]
        return outs[t].at[side, chip_at(at, chips), core, :, pl.ds(cuts[t], wide)]

    def forward(t, at):
        return late(t, dp, at)

    has_late = [t for t in range(count) if outs[t].shape[-1] > cuts[t]]
    crossing = []
    for t in range(count):
        columns = pl.ds(0, cuts[t])
        crossing.append(
            start(ins[t].at[:, columns], outs[t].at[dp, chip, core, :, columns], across)
        )
    for copy in kept:
        copy.wait()

    up_late, down_late = (chips - 1) // 2, chips // 2
    up_early, down_early = chips // 2, (chips - 1) // 2
    landed = []
    crossed = []

    def pass_late(t, at):
        crossed.append((t, at, start(forward(t, at), forward(t, at), across)))
        landed.append(start(forward(t, at), forward(t, at), beside))

    rings = []
    for t in has_late:
        up = start(forward(t, place), forward(t, place), to_ahead)
        down = start(forward(t, place), forward(t, place), to_behind)
        pass_late(t, place)
        rings.append([t, up, down])
    landed += [start(one, two, across) for one, two in zip(singles, singles_out)]
    early_rings = []
    for t in range(count):
        crossing[t].wait_recv()
        up = start(early(t, place), early(t, place), to_ahead)
        down = start(early(t, place), early(t, place), to_behind)
        landed.append(start(early(t, place), early(t, place), beside))
        early_rings.append([t, up, down])
    for hop in range(1, chips // 2 + 1):
        above, below = place + chips - hop, place + hop
        for ring in rings:
            t, up, down = ring
            if hop <= up_late:
                up.wait_recv()
                if hop < up_late:
                    ring[1] = start(forward(t, above), forward(t, above), to_ahead)
                pass_late(t, above)
            if hop <= down_late:
                down.wait_recv()
                if hop < down_late:
                    ring[2] = start(forward(t, below), forward(t, below), to_behind)
                pass_late(t, below)
        for ring in early_rings:
            t, up, down = ring
            if hop <= up_early:
                up.wait_recv()
                if hop < up_early:
                    ring[1] = start(early(t, above), early(t, above), to_ahead)
                landed.append(start(early(t, above), early(t, above), beside))
            if hop <= down_early:
                down.wait_recv()
                if hop < down_early:
                    ring[2] = start(early(t, below), early(t, below), to_behind)
                landed.append(start(early(t, below), early(t, below), beside))
    for t, at, copy in crossed:
        copy.wait_recv()
        landed.append(start(late(t, 1 - dp, at), late(t, 1 - dp, at), beside))
    for copy in landed:
        copy.wait_recv()
    for copy in sent:
        copy.wait_send()


def gather_everywhere(shards_of, cuts, others):
    chips = lax.axis_size("chip")
    slots = len(others)
    for part, cut in zip(shards_of, cuts):
        slots += 2 * chips + (4 * chips - 1 if part.shape[1] > cut else 0)
    arrays = list(shards_of) + list(others)
    outs = [jax.ShapeDtypeStruct((2, chips, 2) + part.shape, part.dtype) for part in shards_of]
    outs += [jax.ShapeDtypeStruct(part.shape, part.dtype) for part in others]
    moved = sum(4 * chips * part.size * 2 for part in shards_of)
    return pl.pallas_call(
        functools.partial(gather_kernel, cuts, len(others)),
        in_specs=[pl.BlockSpec(memory_space=pl.ANY)] * len(arrays),
        out_specs=[pl.BlockSpec(memory_space=pl.ANY)] * len(arrays),
        out_shape=outs,
        scratch_shapes=[
            pltpu.SemaphoreType.DMA((len(shards_of),)),
            pltpu.SemaphoreType.DMA((slots,)),
            pltpu.SemaphoreType.DMA((slots,)),
        ],
        compiler_params=pltpu.CompilerParams(collective_id=0, has_side_effects=True),
        cost_estimate=pl.CostEstimate(flops=0, bytes_accessed=6 * moved, transcendentals=0),
        name="gather_everywhere",
    )(*arrays)


def ring_kernel(cuts, *refs):
    count = len(cuts)
    ins, outs = refs[:count], refs[count : 2 * count]
    slots = [refs[2 * count + 2 * t : 2 * count + 2 * t + 2] for t in range(count)]
    send_sem, recv_sem = refs[4 * count :]
    dp, chip, core = (lax.axis_index(name) for name in ALL)
    chips = lax.axis_size("chip")
    place = place_of(chip, chips)
    ahead, behind = chip_at(place + 1, chips), chip_at(place + chips - 1, chips)
    devices = ((dp, ahead, core), (dp, behind, core))

    barrier = pltpu.get_barrier_semaphore()
    for device in devices:
        pl.semaphore_signal(barrier, inc=1, device_id=device, device_id_type=MESH)
    pl.semaphore_wait(barrier, 2)

    def columns(t, way):
        return pl.ds(0, cuts[t]) if way == 0 else pl.ds(cuts[t], ins[t].shape[-1] - cuts[t])

    def block(t, way, step):
        at = place + 2 * chips - 2 - step if way == 0 else place + 2 + step
        return ins[t].at[chip_at(at, chips), :, columns(t, way)]

    def copy(t, way, step, source):
        return pltpu.make_async_remote_copy(
            src_ref=source,
            dst_ref=slots[t][way].at[step],
            send_sem=send_sem.at[t, way, step],
            recv_sem=recv_sem.at[t, way, step],
            device_id=devices[way],
            device_id_type=MESH,
        )

    pairs = [(t, way) for t in range(count) for way in (0, 1)]
    for t, way in pairs:
        copy(t, way, 0, block(t, way, -1)).start()

    def hop(step, carry):
        for t, way in pairs:
            slot = slots[t][way].at[step - 1]
            copy(t, way, step - 1, slot).wait_recv()
            own = block(t, way, step - 1)[...].astype(jnp.float32)
            slot[...] = (slot[...].astype(jnp.float32) + own).astype(jnp.bfloat16)
            copy(t, way, step, slot).start()
        return carry

    lax.fori_loop(1, chips - 1, hop, 0)
    last = chips - 2
    for t, way in pairs:
        slot = slots[t][way].at[last]
        copy(t, way, last, slot).wait_recv()
        total = slot[...].astype(jnp.float32) + block(t, way, last)[...].astype(jnp.float32)
        outs[t][:, columns(t, way)] = total.astype(outs[t].dtype)

    def finish(step, carry):
        for t, way in pairs:
            copy(t, way, step, slots[t][way].at[step]).wait_send()
        return carry

    lax.fori_loop(0, chips - 1, finish, 0)


def ring_scatter(totals):
    chips = lax.axis_size("chip")
    cuts = [-(-total.shape[2] // (2 * LANES)) * LANES for total in totals]
    vmem = pl.BlockSpec(memory_space=pltpu.VMEM)
    slots = []
    for total, cut in zip(totals, cuts):
        for width in (cut, total.shape[2] - cut):
            slots.append(pltpu.VMEM((chips - 1, total.shape[1], width), jnp.bfloat16))
    return pl.pallas_call(
        functools.partial(ring_kernel, cuts),
        in_specs=[vmem] * len(totals),
        out_specs=[vmem] * len(totals),
        out_shape=[jax.ShapeDtypeStruct(total.shape[1:], jnp.float32) for total in totals],
        scratch_shapes=slots
        + [
            pltpu.SemaphoreType.DMA((len(totals), 2, chips - 1)),
            pltpu.SemaphoreType.DMA((len(totals), 2, chips - 1)),
        ],
        compiler_params=pltpu.CompilerParams(
            collective_id=1, has_side_effects=True, vmem_limit_bytes=VMEM_LIMIT
        ),
        cost_estimate=pl.CostEstimate(
            flops=0, bytes_accessed=sum(8 * total.size for total in totals), transcendentals=0
        ),
        name="ring_scatter",
    )(*totals)


def meet(one, two, bit, send):
    kept, given = jnp.where(bit == 0, one, two), jnp.where(bit == 0, two, one)
    return kept.astype(jnp.float32) + send(given).astype(jnp.float32)


def halve_dp(total):
    columns = total.shape[-1] // 2
    return meet(total[..., :columns], total[..., columns:], lax.axis_index("dp"), swap)


def split_lanes(array):
    half = array.shape[1] // 2
    return jnp.concatenate([pad_lanes(array[:, :half]), pad_lanes(array[:, half:])], axis=1)


def pad_lanes(array):
    columns = array.shape[1]
    return jnp.pad(array, ((0, 0), (0, -columns % LANES)))


def repack_kernel(count, source, target, start, keep, in_ref, out_ref):
    rows = in_ref.shape[0]
    pieces = []
    for block in range(count):
        at = block * source + start
        pieces.append(in_ref[:, at : at + keep].astype(jnp.float32))
        if target > keep:
            pieces.append(jnp.zeros((rows, target - keep), jnp.float32))
    out_ref[...] = jnp.concatenate(pieces, axis=1).astype(out_ref.dtype)


def repack(array, count, source, target, start=0, keep=None):
    keep = min(source, target) if keep is None else keep
    rows = array.shape[0]
    if source == target and keep == source:
        return array
    step = 64 if rows % 64 == 0 else rows
    return pl.pallas_call(
        functools.partial(repack_kernel, count, source, target, start, keep),
        grid=(rows // step,),
        in_specs=[pl.BlockSpec((step, count * source), lambda r: (r, 0))],
        out_specs=pl.BlockSpec((step, count * target), lambda r: (r, 0)),
        out_shape=jax.ShapeDtypeStruct((rows, count * target), array.dtype),
        compiler_params=params(),
        name="repack",
    )(array)


def weave_kernel(count, source, keep, one_ref, two_ref, out_ref):
    pieces = []
    for block in range(count):
        for ref in (one_ref, two_ref):
            pieces.append(ref[:, block * source : block * source + keep].astype(jnp.float32))
    out_ref[...] = jnp.concatenate(pieces, axis=1)


def weave(one, two, count, source, keep):
    rows = one.shape[0]
    return pl.pallas_call(
        functools.partial(weave_kernel, count, source, keep),
        out_shape=jax.ShapeDtypeStruct((rows, 2 * count * keep), jnp.float32),
        compiler_params=pltpu.CompilerParams(vmem_limit_bytes=VMEM_LIMIT),
        name="weave",
    )(one, two)


def convolve(extended, kernel, bias_row):
    length = extended.shape[0] - kernel.shape[1] + 1
    convolved = bias_row
    for offset in range(kernel.shape[1]):
        convolved = convolved + kernel[:, offset] * extended[offset : offset + length, :]
    return convolved


def decay_rates(decay_wide):
    return -jnp.exp(decay_wide.T)


def gating(scanned, gate_path):
    return scanned * silu_gate(gate_path)


def activate(gate_pre, up_pre):
    return silu_gate(gate_pre) * up_pre


def dot(left, right):
    return jnp.dot(left, right, preferred_element_type=jnp.float32)


def dot_rows(left, right):
    return lax.dot_general(left, right, (((0,), (0,)), ((), ())), preferred_element_type=jnp.float32)


def dot_columns(left, right):
    return lax.dot_general(left, right, (((1,), (1,)), ((), ())), preferred_element_type=jnp.float32)


def combine_paths(attended, mamba_path, attention_row, mamba_row):
    return jnp.concatenate(
        [
            rms_norm(attended, attention_row, attended.shape[-1]),
            rms_norm(mamba_path, mamba_row, mamba_path.shape[-1]),
        ],
        axis=-1,
    )


def shards(
    tokens,
    cotangent,
    input_gain,
    merged_weight,
    meta_tokens,
    select_weight,
    step_weight,
    decay_log,
    conv_weight,
    conv_bias,
    step_bias,
    skip_gain,
    attention_gain,
    mamba_gain,
    output_weight,
    second_gain,
    expand_weight,
    down_weight,
):
    parts = lax.axis_size("chip") * lax.axis_size("core")
    position = lax.axis_index(SEQ)
    first = lax.axis_index("dp") == 0
    tokens = tokens[0]
    cotangent = cotangent[0]
    local_len, width = tokens.shape
    query_width = HEADS * HEAD
    key_width = KVHEADS * HEAD
    inner_start = query_width + 2 * key_width
    half = merged_weight.shape[1]
    reach_count = (WINDOW - 1) // local_len + 1
    rows_in = merged_weight.shape[0]
    rows_pad = ceil8(rows_in)
    rows_channel = select_weight.shape[0]
    channel_pad = ceil8(rows_channel)
    rows_joined = output_weight.shape[0]
    joined_pad = ceil8(rows_joined)
    rows_hidden = down_weight.shape[0]
    hidden_half = rows_hidden // 2
    hidden_pad = ceil8(hidden_half)
    hidden_width = parts * hidden_pad
    wide = lambda row: row.astype(jnp.float32)
    conv_bias_wide = wide(conv_bias)
    step_bias_wide = wide(step_bias)
    skip_wide = wide(skip_gain)[None]
    input_row, second_row = wide(input_gain), wide(second_gain)
    attention_row, mamba_row = wide(attention_gain), wide(mamba_gain)

    columns = [weight.shape[1] for weight in (select_weight, step_weight, decay_log, conv_weight)]
    small = jnp.concatenate([select_weight, step_weight, decay_log, conv_weight], axis=1)
    small = jnp.pad(small, ((0, channel_pad - rows_channel), (0, LANES - sum(columns))))
    meta_part = jnp.pad(
        meta_tokens, ((0, rows_pad - rows_in), (0, LANES - meta_tokens.shape[1]))
    )
    small = jnp.concatenate([small, meta_part], axis=0)
    expand_rows = pad_rows(expand_weight, rows_pad)
    expand_halves = [
        repack(expand_rows, parts, rows_hidden, hidden_pad, at, hidden_half)
        for at in (0, hidden_half)
    ]
    down_halves = [
        pad_rows(down_weight[:hidden_half], hidden_pad),
        pad_rows(down_weight[hidden_half:], hidden_pad),
    ]
    cut = output_weight.shape[1]
    merged_full, output_full, small_full, expand_got, down_got, cotangent_got = gather_everywhere(
        [
            pad_lanes(pad_rows(merged_weight, rows_pad)),
            pad_lanes(pad_rows(output_weight, joined_pad)),
            small,
        ],
        (17 * LANES, 4 * LANES, LANES),
        [
            jnp.where(first, expand_halves[1], expand_halves[0]),
            jnp.where(first, down_halves[1], down_halves[0]),
            cotangent,
        ],
    )
    merged_full = merged_full.reshape(2, parts * rows_pad, -1)
    output_full = output_full.reshape(2, parts * joined_pad, -1)
    small_full = small_full.reshape(2, parts, channel_pad + rows_pad, LANES)
    kept = jnp.where(first, expand_halves[0], expand_halves[1])
    expand_mine = jnp.concatenate(
        [jnp.where(first, kept, expand_got), jnp.where(first, expand_got, kept)], axis=1
    )
    kept = jnp.where(first, down_halves[0], down_halves[1])
    down_mine = jnp.concatenate(
        [jnp.where(first, kept, down_got), jnp.where(first, down_got, kept)], axis=1
    )
    small_full, merged_full, expand_mine, down_mine = lax.optimization_barrier(
        (small_full, merged_full, expand_mine, down_mine)
    )
    expand_full = lax.all_gather(expand_mine, SEQ).reshape(parts * rows_pad, 2 * hidden_width)
    down_full = lax.all_gather(down_mine, SEQ).reshape(hidden_width, width)
    cotangent_both = jnp.concatenate([cotangent, cotangent_got], axis=0)
    channel_rows = [part[:, :rows_channel].reshape(MINNER, LANES) for part in small_full]
    pieces, at = [], 0
    for count in columns:
        pieces.append(jnp.concatenate([channel_rows[h][:, at : at + count] for h in (0, 1)], axis=1))
        at += count
    select_full, step_full, decay_full, kernel_full = pieces
    meta_full = jnp.concatenate(
        [
            small_full[h][:, channel_pad:, : meta_tokens.shape[1]].reshape(
                parts * rows_pad, meta_tokens.shape[1]
            )
            for h in (0, 1)
        ],
        axis=1,
    )

    tokens_wide = wide(tokens)
    normed_wide, norm_back = jax.vjp(lambda v, g: rms_norm(v, g, width), tokens_wide, input_row)
    normed = repack(normed_wide.astype(jnp.bfloat16), parts, rows_in, rows_pad)
    input_row_pad = jnp.pad(
        input_row.reshape(parts, rows_in), ((0, 0), (0, rows_pad - rows_in))
    ).reshape(parts * rows_pad)
    meta_wide, meta_back = jax.vjp(
        lambda v, g: rms_norm(v, g, width), wide(meta_full).T, input_row_pad
    )
    stacked_normed = jnp.concatenate([normed, meta_wide.astype(jnp.bfloat16)], axis=0)
    projected_one = dot(stacked_normed, merged_full[0])
    projected_two = dot(normed, merged_full[1])
    queries = projected_one[:local_len, :query_width].astype(jnp.bfloat16)
    pairs_own = projected_one[:local_len, query_width:inner_start].astype(jnp.bfloat16)
    meta_pairs = projected_one[local_len:, query_width:inner_start].astype(jnp.bfloat16)
    inner_path = jnp.concatenate(
        [
            projected_one[:local_len, inner_start:half].astype(jnp.bfloat16),
            projected_two[:, : inner_start + MINNER - half].astype(jnp.bfloat16),
        ],
        axis=1,
    )
    gate_path = projected_two[:, inner_start + MINNER - half : half]

    pairs = jnp.concatenate(
        [meta_pairs]
        + [from_behind(pairs_own, behind) for behind in range(reach_count, 0, -1)]
        + [pairs_own],
        axis=0,
    )
    where = jnp.reshape(position, (1,)).astype(jnp.int32)
    heads_first = lambda rows: jnp.moveaxis(rows.reshape(rows.shape[0], KVHEADS, HEAD), 1, 0)
    keys, values = heads_first(pairs[:, :key_width]), heads_first(pairs[:, key_width:])
    key_turned, value_turned = pairs[:, :key_width].T, pairs[:, key_width:].T
    query_turned = queries.T
    attended_turned, logs = attend(where, query_turned, keys, value_turned, reach_count + 1)
    attended = attended_turned.T

    previous = from_behind(inner_path[local_len - (CONV - 1) :], 1)
    extended = wide(jnp.concatenate([previous, inner_path], axis=0))
    kernel = wide(kernel_full)
    convolved, convolve_back = jax.vjp(convolve, extended, kernel, conv_bias_wide)
    activated, silu_back = jax.vjp(silu_gate, convolved)
    signal = activated.astype(jnp.bfloat16)
    selected = dot(signal, select_full)
    step_raw = selected[:, :DTR].astype(jnp.bfloat16)
    spread_lanes = lambda mix: jnp.broadcast_to(mix[:, :, None], (local_len, STATE, LANES))
    write_wide = spread_lanes(selected[:, DTR : DTR + STATE])
    read_wide = spread_lanes(selected[:, DTR + STATE :])
    step_pre = dot_columns(step_raw, step_full) + step_bias_wide
    step_size = softplus(step_pre)
    decays, decay_back = jax.vjp(decay_rates, wide(decay_full))
    ends = scan_ends(step_size, signal, write_wide, decays)
    ends, expand_full = lax.optimization_barrier((ends, expand_full))
    carried = lax.all_gather(
        jnp.concatenate([ends, jnp.sum(step_size, axis=0, keepdims=True)], axis=0), SEQ
    )
    totals = carried[:, STATE:]
    scanned, enter = scan_forward(
        where, step_size, signal, write_wide, read_wide, decays, skip_wide, totals, carried[:, :STATE]
    )
    mamba_path, gating_back = jax.vjp(gating, scanned, gate_path)
    joined_wide, paths_back = jax.vjp(
        combine_paths, attended, mamba_path, attention_row, mamba_row
    )
    joined = repack(joined_wide.astype(jnp.bfloat16), parts, rows_joined, joined_pad)
    hidden = tokens_wide + 0.5 * jnp.concatenate(
        [dot(joined, output_full[0])[:, :cut], dot(joined, output_full[1])[:, :cut]], axis=1
    )

    normed_two_wide, norm_two_back = jax.vjp(lambda v, g: rms_norm(v, g, width), hidden, second_row)
    normed_two = repack(normed_two_wide.astype(jnp.bfloat16), parts, rows_in, rows_pad)
    normed_both = jnp.concatenate([normed_two, swap(normed_two)], axis=0)
    expanded = dot(normed_both, expand_full)
    active_wide, activate_back = jax.vjp(
        activate, expanded[:, :hidden_width], expanded[:, hidden_width:]
    )
    active = active_wide.astype(jnp.bfloat16)
    down_out = dot(active, down_full)
    block_output = (
        hidden + down_out[:local_len] + wide(swap(down_out[local_len:].astype(jnp.bfloat16)))
    ).astype(jnp.bfloat16)

    hidden_columns = parity_columns(active, parts, hidden_pad)
    down_grad = grad_parts(hidden_columns, pad_lanes(cotangent_both))
    down_sum = scatter_rows(down_grad, hidden_pad)
    active_grad = dot_columns(cotangent_both, down_full)
    gate_grad, up_grad = activate_back(active_grad)
    expand_in = jnp.concatenate(
        [gate_grad.astype(jnp.bfloat16), up_grad.astype(jnp.bfloat16)], axis=1
    )
    second_both = dot_columns(expand_in, expand_full)
    second_normed_grad = repack(
        second_both[:local_len] + wide(swap(second_both[local_len:].astype(jnp.bfloat16))),
        parts,
        rows_pad,
        rows_in,
    )
    hidden_part, second_gain_grad = norm_two_back(second_normed_grad)
    hidden_grad = hidden_part + wide(cotangent)
    mixed_in = hidden_grad.astype(jnp.bfloat16)
    mixed_split = split_lanes(mixed_in)
    cut_pad = mixed_split.shape[1] // 2
    joined_grad = repack(
        0.5
        * (
            dot_columns(mixed_split[:, :cut_pad], output_full[0])
            + dot_columns(mixed_split[:, cut_pad:], output_full[1])
        ),
        parts,
        joined_pad,
        rows_joined,
    )
    attended_grad, mamba_grad, attention_gain_grad, mamba_gain_grad = paths_back(joined_grad)
    scanned_grad, gate_path_grad = gating_back(mamba_grad)
    own_pull = scan_pulls(step_size, scanned_grad, read_wide, decays)
    pulls = lax.all_gather(own_pull, SEQ)

    normed_both, joined, own_pull, down_sum = lax.optimization_barrier(
        (normed_both, joined, own_pull, down_sum)
    )
    both_split = parity_columns(normed_both, parts, rows_pad)
    gate_total = grad_parts(both_split, expand_in[:, :hidden_width])
    up_total = grad_parts(both_split, expand_in[:, hidden_width:])
    output_grad = grad_parts(parity_columns(joined, parts, joined_pad), mixed_split, 0.5)
    attended_in, gate_total, up_total, output_grad, pulls = lax.optimization_barrier(
        (attended_grad.astype(jnp.bfloat16), gate_total, up_total, output_grad, pulls)
    )
    gate_sum = scatter_rows(gate_total, rows_pad)
    up_sum = scatter_rows(up_total, rows_pad)
    output_grad = halve_dp(output_grad).astype(jnp.bfloat16)
    output_sum = scatter_rows(output_grad, joined_pad)

    query_grad_turned, key_grads, value_grads = attend_back(
        where,
        query_turned,
        attended_in.T,
        attended_turned,
        logs,
        keys,
        values,
        key_turned,
        reach_count + 1,
    )
    heads_last = lambda grads: jnp.moveaxis(grads, 0, 1).reshape(grads.shape[1], key_width)
    pair_grads = jnp.concatenate([heads_last(key_grads), heads_last(value_grads)], axis=1)
    meta_pair_grad, window_grad = pair_grads[:META], pair_grads[META:]
    own_grad = window_grad[reach_count * local_len :]
    for behind in range(1, reach_count + 1):
        own_grad = own_grad + wide(
            from_behind(
                window_grad[
                    (reach_count - behind) * local_len : (reach_count - behind + 1) * local_len
                ].astype(jnp.bfloat16),
                -behind,
            )
        )

    own_grad, meta_pair_grad, gate_sum = lax.optimization_barrier(
        (own_grad, meta_pair_grad, gate_sum)
    )
    with_meta = lambda rows, meta: jnp.concatenate([rows, meta], axis=0)
    query_in = with_meta(query_grad_turned.T, jnp.zeros((META, query_width), jnp.bfloat16))
    pair_in = with_meta(own_grad, meta_pair_grad).astype(jnp.bfloat16)
    gate_in = with_meta(gate_path_grad.astype(jnp.bfloat16), jnp.zeros((META, MINNER), jnp.bfloat16))
    normed_split = parity_columns(stacked_normed, parts, rows_pad)
    early_grad = grad_parts(
        normed_split, pad_lanes(jnp.concatenate([gate_in, query_in, pair_in], axis=1))
    )
    scanned_grad, early_grad = lax.optimization_barrier((scanned_grad, early_grad))
    gate_early = early_grad[:, :MINNER]
    pair_early = jnp.pad(
        early_grad[:, MINNER : MINNER + inner_start], ((0, 0), (0, MINNER - inner_start))
    )
    early_grad = meet(pair_early, gate_early, lax.axis_index("dp"), swap).astype(jnp.bfloat16)
    signal_grad, step_grad, write_parts, read_parts, decays_grad, skip_parts = scan_backward(
        where,
        step_size,
        signal,
        scanned_grad,
        write_wide,
        read_wide,
        decays,
        skip_wide,
        enter,
        totals,
        pulls,
    )
    step_grad, up_sum = lax.optimization_barrier((step_grad, up_sum))
    step_pre_grad = step_grad * jax.nn.sigmoid(step_pre)
    step_in = step_pre_grad.astype(jnp.bfloat16)
    step_weight_grad = dot_rows(step_in, step_raw)
    selected_in = jnp.concatenate(
        [dot(step_in, step_full), jnp.sum(write_parts, axis=-1), jnp.sum(read_parts, axis=-1)],
        axis=-1,
    ).astype(jnp.bfloat16)
    select_grad = dot_rows(signal, selected_in)
    signal_grad = signal_grad + dot_columns(selected_in, select_full)
    extended_grad, kernel_grad, conv_bias_grad = convolve_back(silu_back(signal_grad)[0])
    returned_tail = wide(from_behind(extended_grad[: CONV - 1].astype(jnp.bfloat16), -1))
    inner_grad = extended_grad[CONV - 1 :] + jnp.pad(
        returned_tail, ((local_len - (CONV - 1), 0), (0, 0))
    )
    decay_grad = decay_back(decays_grad)[0]

    inner_in = with_meta(inner_grad.astype(jnp.bfloat16), jnp.zeros((META, MINNER), jnp.bfloat16))
    inner_in, output_sum = lax.optimization_barrier((inner_in, output_sum))
    inner_cut = half - inner_start
    inner_first = -(-inner_cut // LANES) * LANES
    inner_grads = grad_parts(
        normed_split,
        jnp.concatenate([pad_lanes(inner_in[:, :inner_cut]), pad_lanes(inner_in[:, inner_cut:])], axis=1),
    )
    one_in = pad_lanes(jnp.concatenate([query_in, pair_in, inner_in[:, :inner_cut]], axis=1))
    two_in = pad_lanes(
        jnp.concatenate([inner_in[:local_len, inner_cut:], gate_in[:local_len]], axis=1)
    )
    stacked_grad = dot_columns(one_in, merged_full[0])
    normed_grad = repack(
        stacked_grad[:local_len] + dot_columns(two_in, merged_full[1]), parts, rows_pad, rows_in
    )
    meta_rows_grad, meta_gain_grad = meta_back(stacked_grad[local_len:])
    tokens_part, input_gain_part = norm_back(normed_grad)
    tokens_grad = hidden_grad + tokens_part
    input_gain_grad = input_gain_part + (
        meta_gain_grad.reshape(parts, rows_pad)[:, :rows_in].reshape(width)
    )

    count = meta_tokens.shape[1]
    meta_grads = jnp.pad(
        meta_rows_grad.T.reshape(parts, rows_pad, META),
        ((0, 0), (0, channel_pad - rows_pad), (0, 0)),
    )
    sides = []
    for h in (0, 1):
        cuts = [
            grad[:, h * size : (h + 1) * size]
            for grad, size in zip((select_grad, step_weight_grad, decay_grad, kernel_grad), columns)
        ]
        side = jnp.concatenate(cuts, axis=1).reshape(parts, rows_channel, sum(columns))
        side = jnp.pad(
            side, ((0, 0), (0, channel_pad - rows_channel), (0, LANES - sum(columns)))
        )
        meta_side = meta_grads[:, :, h * count : (h + 1) * count]
        sides += [side, jnp.pad(meta_side, ((0, 0), (0, 0), (0, LANES - count)))]
    small_grads = jnp.concatenate(sides, axis=2).astype(jnp.bfloat16)
    small_grads = small_grads.reshape(parts // 2, 2, channel_pad, 4 * LANES)
    small_sum = meet(
        small_grads[:, 0],
        small_grads[:, 1],
        lax.axis_index("core"),
        lambda array: swap(array, "core"),
    )
    inner_sum, early_out, small_sum = ring_scatter(
        [
            inner_grads.reshape(parts // 2, rows_pad, -1),
            early_grad.reshape(parts // 2, rows_pad, -1),
            small_sum.astype(jnp.bfloat16),
        ]
    )
    output_out = wide(output_sum)[:rows_joined, :cut]
    early_out = early_out[:rows_in]
    small_sum = halve_dp(small_sum)
    inner_one, inner_two = inner_sum[:, :inner_first], inner_sum[:, inner_first:]
    inner_two = jnp.pad(inner_two, ((0, 0), (0, inner_first - inner_two.shape[1])))
    inner_out = meet(
        inner_one, inner_two, lax.axis_index("dp"), lambda array: swap(array.astype(jnp.bfloat16))
    )[:rows_in]
    small_outs, at = [], 0
    for size in columns:
        small_outs.append(small_sum[:rows_channel, at : at + size])
        at += size
    meta_sum = small_sum[:rows_in, LANES : LANES + count]

    vectors = (
        second_gain_grad,
        attention_gain_grad,
        mamba_gain_grad,
        jnp.sum(skip_parts, axis=0),
        jnp.sum(step_pre_grad, axis=0),
        conv_bias_grad,
        input_gain_grad,
    )
    flat = jnp.concatenate(vectors)
    padded = -(-flat.shape[0] // (8 * LANES)) * 8 * LANES
    flat = sum_everywhere(jnp.pad(flat, (0, padded - flat.shape[0])).reshape(-1, LANES))
    flat = flat.reshape(-1)
    sums, at = [], 0
    for vector in vectors:
        sums.append(flat[at : at + vector.shape[0]])
        at += vector.shape[0]

    rest = half - MINNER
    merged_out = jnp.where(
        first,
        jnp.concatenate([early_out[:, :inner_start], inner_out[:, :inner_cut]], axis=1),
        jnp.concatenate([inner_out[:, :rest], early_out], axis=1),
    )
    gate_part, up_part = gate_sum, up_sum
    kept = jnp.where(first, gate_part, up_part)
    got = swap(jnp.where(first, up_part, gate_part))
    expand_out = weave(
        jnp.where(first, kept, got), jnp.where(first, got, kept), parts, hidden_pad, hidden_half
    )[:rows_in]
    kept = jnp.where(first, down_sum[:, :cut], down_sum[:, cut : 2 * cut])
    got = swap(jnp.where(first, down_sum[:, cut : 2 * cut], down_sum[:, :cut]))
    down_out_grad = jnp.concatenate(
        [
            jnp.where(first, kept, got)[:hidden_half],
            jnp.where(first, got, kept)[:hidden_half],
        ],
        axis=0,
    )
    return (
        block_output[None],
        tokens_grad[None],
        sums[6],
        merged_out,
        meta_sum,
        small_outs[0],
        small_outs[1],
        small_outs[2],
        small_outs[3],
        sums[5],
        sums[4],
        sums[3],
        sums[1],
        sums[2],
        output_out,
        sums[0],
        expand_out,
        wide(down_out_grad),
    )


def solution(mesh):
    split = Mesh(mesh.devices.reshape(2, -1, 2), ALL)
    rows, matrix, copied = P("dp", SEQ, None), P(SEQ, "dp"), P()
    return jax.shard_map(
        shards,
        mesh=split,
        in_specs=(rows, rows, copied) + (matrix,) * 6 + (copied,) * 5 + (matrix, copied, matrix, matrix),
        out_specs=(rows, rows, copied) + (matrix,) * 6 + (copied,) * 5 + (matrix, copied, matrix, matrix),
        check_vma=False,
    )
```

```python
import functools

import jax
import jax.numpy as jnp
from jax import lax
from jax.experimental import pallas as pl
from jax.experimental.pallas import tpu as pltpu
from jax.sharding import Mesh
from jax.sharding import PartitionSpec as P

HEADS = 25
KVHEADS = 5
HEAD = 64
MINNER = 3200
STATE = 16
DTR = 100
META = 128
WINDOW = 1024
CONV = 4
epsilon = 1e-06
LANES = 128
STEPS = 8
LOG2E = 1.4426950408889634
VMEM_LIMIT = 60 * 1024 * 1024


def lane_tiles(width):
    return [slice(at, min(at + LANES, width)) for at in range(0, width, LANES)]


def chunk_of(channels):
    for tiles in (5, 4, 6, 3, 2, 7, 1):
        if channels % (tiles * LANES) == 0:
            return tiles * LANES
    return channels


def fold(rows):
    sub = lax.broadcasted_iota(jnp.int32, rows[0].shape, 0)
    for bit in (1, 2, 4):
        clear = (sub & bit) == 0
        rows = [
            jnp.where(clear, one, two) + pltpu.roll(jnp.where(clear, two, one), bit, 0)
            for one, two in zip(rows[0::2], rows[1::2])
        ]
    return rows[0]


def halves(product):
    return product[:8] + product[8:]


def ends_kernel(step_ref, signal_ref, write_ref, decay_ref, end_ref):
    length, width = step_ref.shape
    tiles = lane_tiles(width)
    rates = [decay_ref[:, tile] * LOG2E for tile in tiles]

    def block(at, states):
        states = list(states)
        rows = pl.ds(pl.multiple_of(at * STEPS, STEPS), STEPS)
        step = step_ref[rows, :]
        drive = step * signal_ref[rows, :].astype(jnp.float32)
        for i in range(STEPS):
            write = write_ref[at * STEPS + i]
            for j, tile in enumerate(tiles):
                factor = jnp.exp2(step[i : i + 1, tile] * rates[j])
                states[j] = factor * states[j] + drive[i : i + 1, tile] * write[:, : tile.stop - tile.start]
        return tuple(states)

    zero = tuple(jnp.zeros((STATE, tile.stop - tile.start), jnp.float32) for tile in tiles)
    final = lax.fori_loop(0, length // STEPS, block, zero)
    for j, tile in enumerate(tiles):
        end_ref[:, tile] = final[j]


def pull_kernel(step_ref, grad_ref, read_ref, decay_ref, end_ref):
    length, width = step_ref.shape
    tiles = lane_tiles(width)
    rates = [decay_ref[:, tile] * LOG2E for tile in tiles]
    blocks = length // STEPS

    def block(k, states):
        at = blocks - 1 - k
        states = list(states)
        rows = pl.ds(pl.multiple_of(at * STEPS, STEPS), STEPS)
        step = step_ref[rows, :]
        grad = grad_ref[rows, :]
        for i in reversed(range(STEPS)):
            read = read_ref[at * STEPS + i]
            for j, tile in enumerate(tiles):
                factor = jnp.exp2(step[i : i + 1, tile] * rates[j])
                states[j] = factor * (states[j] + grad[i : i + 1, tile] * read[:, : tile.stop - tile.start])
        return tuple(states)

    zero = tuple(jnp.zeros((STATE, tile.stop - tile.start), jnp.float32) for tile in tiles)
    final = lax.fori_loop(0, blocks, block, zero)
    for j, tile in enumerate(tiles):
        end_ref[:, tile] = final[j]


def carry_over(position, count, reverse, rates, totals_ref, ends_ref, tile):
    def step(k, state):
        at = count - 1 - k if reverse else k
        reached = at > position if reverse else at < position
        factor = jnp.exp2(totals_ref[at, :, tile] * rates)
        new = factor * state + ends_ref[at, :, tile].astype(jnp.float32)
        return jnp.where(reached, new, state)

    return lax.fori_loop(0, count, step, jnp.zeros(rates.shape, jnp.float32))


def scan_kernel(
    position_ref, step_ref, signal_ref, write_ref, read_ref, decay_ref, skip_ref,
    totals_ref, ends_ref, out_ref, enter_ref,
):
    length, width = step_ref.shape
    tiles = lane_tiles(width)
    rates = [decay_ref[:, tile] * LOG2E for tile in tiles]
    enter = tuple(
        carry_over(position_ref[0], totals_ref.shape[0], False, rates[j], totals_ref, ends_ref, tile)
        for j, tile in enumerate(tiles)
    )
    for j, tile in enumerate(tiles):
        enter_ref[:, tile] = enter[j]

    def block(at, states):
        states = list(states)
        rows = pl.ds(pl.multiple_of(at * STEPS, STEPS), STEPS)
        step = step_ref[rows, :]
        signal = signal_ref[rows, :].astype(jnp.float32)
        drive = step * signal
        parts = [[] for tile in tiles]
        for i in range(STEPS):
            write = write_ref[at * STEPS + i]
            read = read_ref[at * STEPS + i]
            for j, tile in enumerate(tiles):
                wide = tile.stop - tile.start
                factor = jnp.exp2(step[i : i + 1, tile] * rates[j])
                states[j] = factor * states[j] + drive[i : i + 1, tile] * write[:, :wide]
                parts[j].append(halves(read[:, :wide] * states[j]))
        for j, tile in enumerate(tiles):
            out_ref[rows, tile] = fold(parts[j]) + skip_ref[:, tile] * signal[:, tile]
        return tuple(states)

    lax.fori_loop(0, length // STEPS, block, enter)


def scan_back_kernel(
    position_ref, step_ref, signal_ref, grad_ref, write_ref, read_ref, decay_ref, skip_ref,
    enter_ref, totals_ref, pulls_ref,
    signal_grad_ref, step_grad_ref, write_grad_ref, read_grad_ref, decay_grad_ref, skip_grad_ref,
    states_ref, factors_ref,
):
    length, width = step_ref.shape
    tiles = lane_tiles(width)
    blocks = length // STEPS
    decays = [decay_ref[:, tile] for tile in tiles]

    @pl.when(pl.program_id(0) == 0)
    def _():
        write_grad_ref[...] = jnp.zeros_like(write_grad_ref)
        read_grad_ref[...] = jnp.zeros_like(read_grad_ref)

    rates = [decay * LOG2E for decay in decays]
    states_ref[0] = enter_ref[...]

    def forward(at, states):
        states = list(states)
        rows = pl.ds(pl.multiple_of(at * STEPS, STEPS), STEPS)
        step = step_ref[rows, :]
        drive = step * signal_ref[rows, :].astype(jnp.float32)
        for i in range(STEPS):
            write = write_ref[at * STEPS + i]
            for j, tile in enumerate(tiles):
                factor = jnp.exp2(step[i : i + 1, tile] * rates[j])
                states[j] = factor * states[j] + drive[i : i + 1, tile] * write[:, : tile.stop - tile.start]
                factors_ref[at * STEPS + i, :, tile] = factor
                states_ref[at * STEPS + i + 1, :, tile] = states[j]
        return tuple(states)

    lax.fori_loop(0, blocks, forward, tuple(enter_ref[:, tile] for tile in tiles))

    leaving = tuple(
        carry_over(position_ref[0], totals_ref.shape[0], True, rates[j], totals_ref, pulls_ref, tile)
        for j, tile in enumerate(tiles)
    )
    zero = tuple(jnp.zeros_like(decay) for decay in decays)
    zero_row = tuple(jnp.zeros((STEPS, tile.stop - tile.start), jnp.float32) for tile in tiles)

    def backward(k, carry):
        at = blocks - 1 - k
        adjoint, decay_sum, skip_sum = (list(part) for part in carry)
        rows = pl.ds(pl.multiple_of(at * STEPS, STEPS), STEPS)
        step = step_ref[rows, :]
        signal = signal_ref[rows, :].astype(jnp.float32)
        grad = grad_ref[rows, :]
        drive = step * signal
        by_write = [[None] * STEPS for tile in tiles]
        by_decay = [[None] * STEPS for tile in tiles]
        for i in reversed(range(STEPS)):
            write = write_ref[at * STEPS + i]
            read = read_ref[at * STEPS + i]
            write_sum = None
            read_sum = None
            for j, tile in enumerate(tiles):
                wide = tile.stop - tile.start
                row = grad[i : i + 1, tile]
                whole = adjoint[j] + read[:, :wide] * row
                adjoint[j] = factors_ref[at * STEPS + i, :, tile] * whole
                kept = adjoint[j] * states_ref[at * STEPS + i, :, tile]
                decay_sum[j] = decay_sum[j] + step[i : i + 1, tile] * kept
                by_decay[j][i] = halves(decays[j] * kept)
                by_write[j][i] = halves(write[:, :wide] * whole)
                write_part = drive[i : i + 1, tile] * whole
                read_part = row * states_ref[at * STEPS + i + 1, :, tile]
                write_sum = write_part if write_sum is None else write_sum + write_part
                read_sum = read_part if read_sum is None else read_sum + read_part
            write_grad_ref[at * STEPS + i] += write_sum
            read_grad_ref[at * STEPS + i] += read_sum
        for j, tile in enumerate(tiles):
            written = fold(by_write[j])
            signal_grad_ref[rows, tile] = step[:, tile] * written + skip_ref[:, tile] * grad[:, tile]
            step_grad_ref[rows, tile] = signal[:, tile] * written + fold(by_decay[j])
            skip_sum[j] = skip_sum[j] + grad[:, tile] * signal[:, tile]
        return tuple(adjoint), tuple(decay_sum), tuple(skip_sum)

    carry = lax.fori_loop(0, blocks, backward, (leaving, zero, zero_row))
    for j, tile in enumerate(tiles):
        decay_grad_ref[:, tile] = carry[1][j]
        skip_grad_ref[:, tile] = carry[2][j]


def by_chunk(rows, chunk):
    return pl.BlockSpec((rows, chunk), lambda c: (0, c))


def stacked(count, rows, chunk):
    return pl.BlockSpec((count, rows, chunk), lambda c: (0, 0, c))


def whole(shape):
    return pl.BlockSpec(shape, lambda c: (0,) * len(shape))


def params():
    return pltpu.CompilerParams(vmem_limit_bytes=VMEM_LIMIT, dimension_semantics=("arbitrary",))


def scan_ends(step_size, signal, write_wide, decays):
    length, channels = step_size.shape
    chunk = chunk_of(channels)
    return pl.pallas_call(
        ends_kernel,
        grid=(channels // chunk,),
        in_specs=[by_chunk(length, chunk), by_chunk(length, chunk), whole(write_wide.shape), by_chunk(STATE, chunk)],
        out_specs=by_chunk(STATE, chunk),
        out_shape=jax.ShapeDtypeStruct((STATE, channels), jnp.float32),
        compiler_params=params(),
        name="scan_ends",
    )(step_size, signal, write_wide, decays)


def scan_pulls(step_size, grad, read_wide, decays):
    length, channels = step_size.shape
    chunk = chunk_of(channels)
    return pl.pallas_call(
        pull_kernel,
        grid=(channels // chunk,),
        in_specs=[by_chunk(length, chunk), by_chunk(length, chunk), whole(read_wide.shape), by_chunk(STATE, chunk)],
        out_specs=by_chunk(STATE, chunk),
        out_shape=jax.ShapeDtypeStruct((STATE, channels), jnp.float32),
        compiler_params=params(),
        name="scan_pulls",
    )(step_size, grad, read_wide, decays)


def scan_forward(position, step_size, signal, write_wide, read_wide, decays, skip, totals, ends):
    length, channels = step_size.shape
    chunk = chunk_of(channels)
    parts = totals.shape[0]
    return pl.pallas_call(
        scan_kernel,
        grid=(channels // chunk,),
        in_specs=[
            pl.BlockSpec(memory_space=pltpu.SMEM),
            by_chunk(length, chunk), by_chunk(length, chunk), whole(write_wide.shape), whole(read_wide.shape),
            by_chunk(STATE, chunk), by_chunk(1, chunk), stacked(parts, 1, chunk), stacked(parts, STATE, chunk),
        ],
        out_specs=[by_chunk(length, chunk), by_chunk(STATE, chunk)],
        out_shape=[
            jax.ShapeDtypeStruct((length, channels), jnp.float32),
            jax.ShapeDtypeStruct((STATE, channels), jnp.float32),
        ],
        compiler_params=params(),
        name="scan_forward",
    )(position, step_size, signal, write_wide, read_wide, decays, skip, totals, ends)


def scan_backward(position, step_size, signal, grad, write_wide, read_wide, decays, skip, enter, totals, pulls):
    length, channels = step_size.shape
    chunk = chunk_of(channels)
    parts = totals.shape[0]
    return pl.pallas_call(
        scan_back_kernel,
        grid=(channels // chunk,),
        in_specs=[
            pl.BlockSpec(memory_space=pltpu.SMEM),
            by_chunk(length, chunk), by_chunk(length, chunk), by_chunk(length, chunk),
            whole(write_wide.shape), whole(read_wide.shape),
            by_chunk(STATE, chunk), by_chunk(1, chunk), by_chunk(STATE, chunk), stacked(parts, 1, chunk),
            stacked(parts, STATE, chunk),
        ],
        out_specs=[
            by_chunk(length, chunk), by_chunk(length, chunk), whole(write_wide.shape), whole(read_wide.shape),
            by_chunk(STATE, chunk), by_chunk(STEPS, chunk),
        ],
        out_shape=[
            jax.ShapeDtypeStruct((length, channels), jnp.float32),
            jax.ShapeDtypeStruct((length, channels), jnp.float32),
            jax.ShapeDtypeStruct(write_wide.shape, jnp.float32),
            jax.ShapeDtypeStruct(read_wide.shape, jnp.float32),
            jax.ShapeDtypeStruct((STATE, channels), jnp.float32),
            jax.ShapeDtypeStruct((STEPS, channels), jnp.float32),
        ],
        scratch_shapes=[
            pltpu.VMEM((length + 1, STATE, chunk), jnp.float32),
            pltpu.VMEM((length, STATE, chunk), jnp.float32),
        ],
        compiler_params=params(),
        name="scan_backward",
    )(position, step_size, signal, grad, write_wide, read_wide, decays, skip, enter, totals, pulls)


def key_blocks(keys, span, count):
    meta = keys - count * span
    return [(0, meta, None)] + [(meta + b * span, span, b) for b in range(count)]


def masked(scores, place, count, position, other):
    if place is None:
        return scores
    row = lax.broadcasted_iota(jnp.int32, scores.shape, 0)
    column = lax.broadcasted_iota(jnp.int32, scores.shape, 1)
    if place == count - 1:
        return jnp.where(row <= column, scores, other)
    there = position + place >= count - 1
    if place == 0:
        return jnp.where((row > column) & there, scores, other)
    return jnp.where(there, scores, other)


def attend_kernel(count, position_ref, query_ref, key_ref, value_ref, out_ref, log_ref):
    position = position_ref[0]
    span = query_ref.shape[1]
    group = query_ref.shape[0] // HEAD
    blocks = key_blocks(key_ref.shape[1], span, count)
    for head in range(group):
        rows = slice(head * HEAD, (head + 1) * HEAD)
        query = query_ref[rows, :] * (HEAD**-0.5)
        scores = [
            masked(
                jnp.dot(key_ref[0, at : at + size, :], query, preferred_element_type=jnp.float32),
                place, count, position, -1e30,
            )
            for at, size, place in blocks
        ]
        top = functools.reduce(jnp.maximum, [jnp.max(part, axis=0, keepdims=True) for part in scores])
        powers = [jnp.exp(part - top) for part in scores]
        total = sum(jnp.sum(part, axis=0, keepdims=True) for part in powers)
        out = sum(
            jnp.dot(value_ref[:, at : at + size], part.astype(jnp.bfloat16), preferred_element_type=jnp.float32)
            for (at, size, place), part in zip(blocks, powers)
        )
        out_ref[rows, :] = out / total
        log_ref[0, head : head + 1, :] = top + jnp.log(total)


def attend_back_kernel(
    count, position_ref, query_ref, grad_ref, out_ref, log_ref, key_ref, value_ref, key_turned_ref,
    query_grad_ref, key_grad_ref, value_grad_ref,
):
    position = position_ref[0]
    span = query_ref.shape[1]
    group = query_ref.shape[0] // HEAD
    blocks = key_blocks(key_ref.shape[1], span, count)
    turned = (((1,), (1,)), ((), ()))
    for head in range(group):
        rows = slice(head * HEAD, (head + 1) * HEAD)
        query = query_ref[rows, :] * (HEAD**-0.5)
        grad = grad_ref[rows, :]
        along = jnp.sum(grad.astype(jnp.float32) * out_ref[rows, :], axis=0, keepdims=True)
        log_total = log_ref[0, head : head + 1, :]
        query_sum = jnp.zeros((HEAD, span), jnp.float32)
        for at, size, place in blocks:
            keys = slice(at, at + size)
            score = jnp.dot(key_ref[0, keys, :], query, preferred_element_type=jnp.float32)
            prob = jnp.exp(masked(score, place, count, position, -1e30) - log_total)
            prob_grad = jnp.dot(value_ref[0, keys, :], grad, preferred_element_type=jnp.float32)
            score_grad = (prob * (prob_grad - along)).astype(jnp.bfloat16)
            query_sum += jnp.dot(key_turned_ref[:, keys], score_grad, preferred_element_type=jnp.float32)
            by_key = lax.dot_general(score_grad, query, turned, preferred_element_type=jnp.float32)
            by_value = lax.dot_general(prob.astype(jnp.bfloat16), grad, turned, preferred_element_type=jnp.float32)
            if head == 0:
                key_grad_ref[0, keys, :] = by_key
                value_grad_ref[0, keys, :] = by_value
            else:
                key_grad_ref[0, keys, :] += by_key
                value_grad_ref[0, keys, :] += by_value
        query_grad_ref[rows, :] = (query_sum * (HEAD**-0.5)).astype(query_grad_ref.dtype)


def by_head(rows, columns):
    return pl.BlockSpec((rows, columns), lambda g: (g, 0))


def head_stack(rows, columns):
    return pl.BlockSpec((1, rows, columns), lambda g: (g, 0, 0))


def attend(position, query_turned, keys, value_turned, count):
    span = query_turned.shape[1]
    group = query_turned.shape[0] // KVHEADS
    total = keys.shape[1]
    return pl.pallas_call(
        functools.partial(attend_kernel, count),
        grid=(KVHEADS,),
        in_specs=[
            pl.BlockSpec(memory_space=pltpu.SMEM),
            by_head(group, span), head_stack(total, HEAD), by_head(HEAD, total),
        ],
        out_specs=[by_head(group, span), head_stack(8, span)],
        out_shape=[
            jax.ShapeDtypeStruct(query_turned.shape, jnp.float32),
            jax.ShapeDtypeStruct((KVHEADS, 8, span), jnp.float32),
        ],
        compiler_params=params(),
        name="attend",
    )(position, query_turned, keys, value_turned)


def attend_back(position, query_turned, grad_turned, out_turned, logs, keys, values, key_turned, count):
    span = query_turned.shape[1]
    group = query_turned.shape[0] // KVHEADS
    total = keys.shape[1]
    return pl.pallas_call(
        functools.partial(attend_back_kernel, count),
        grid=(KVHEADS,),
        in_specs=[
            pl.BlockSpec(memory_space=pltpu.SMEM),
            by_head(group, span), by_head(group, span), by_head(group, span), head_stack(8, span),
            head_stack(total, HEAD), head_stack(total, HEAD), by_head(HEAD, total),
        ],
        out_specs=[by_head(group, span), head_stack(total, HEAD), head_stack(total, HEAD)],
        out_shape=[
            jax.ShapeDtypeStruct(query_turned.shape, jnp.bfloat16),
            jax.ShapeDtypeStruct(keys.shape, jnp.float32),
            jax.ShapeDtypeStruct(keys.shape, jnp.float32),
        ],
        compiler_params=params(),
        name="attend_back",
    )(position, query_turned, grad_turned, out_turned, logs, keys, values, key_turned)


SEQ = ("chip", "core")
ALL = ("dp",) + SEQ


def from_behind(array, by):
    size = lax.axis_size("chip") * lax.axis_size("core")
    pairs = [(i, i + by) for i in range(size) if 0 <= i + by < size]
    return lax.ppermute(array, SEQ, pairs)


def swap(array, axis="dp"):
    return lax.ppermute(array, axis, [(0, 1), (1, 0)])


def sum_everywhere(array):
    array = array + swap(array, "core")
    chips = lax.axis_size("chip")
    step = 1
    while step < chips:
        array = array + lax.ppermute(array, "chip", [(i, i ^ step) for i in range(chips)])
        step *= 2
    return array + swap(array)


def parity_kernel(parts, block, core_ref, in_ref, own_ref, other_ref):
    values = in_ref[...].astype(jnp.float32)
    even, odd = [
        jnp.concatenate(
            [values[:, at * block : (at + 1) * block] for at in range(core, parts, 2)], axis=1
        )
        for core in (0, 1)
    ]
    own = core_ref[0] == 0
    own_ref[...] = jnp.where(own, even, odd).astype(own_ref.dtype)
    other_ref[...] = jnp.where(own, odd, even).astype(other_ref.dtype)


def parity_columns(array, parts, block):
    rows = array.shape[0]
    step = 64 if rows % 64 == 0 else rows
    half = pl.BlockSpec((step, parts // 2 * block), lambda r: (r, 0))
    return pl.pallas_call(
        functools.partial(parity_kernel, parts, block),
        grid=(rows // step,),
        in_specs=[
            pl.BlockSpec(memory_space=pltpu.SMEM),
            pl.BlockSpec((step, parts * block), lambda r: (r, 0)),
        ],
        out_specs=[half, half],
        out_shape=[jax.ShapeDtypeStruct((rows, parts // 2 * block), array.dtype)] * 2,
        compiler_params=params(),
        name="parity_columns",
    )(jnp.reshape(lax.axis_index("core"), (1,)).astype(jnp.int32), array)


def grad_parts(left, right, scale=1.0):
    kept, given = left
    sent = (scale * dot_rows(given, right)).astype(jnp.bfloat16)
    got = swap(sent, "core")
    return (scale * dot_rows(kept, right) + got.astype(jnp.float32)).astype(jnp.bfloat16)


def scatter_rows(total, rows):
    chips = lax.axis_size("chip")
    return lax.psum_scatter(total.reshape(chips, rows, -1), "chip", scatter_dimension=0)


def rms_norm(values, gain_row, count):
    mean = jnp.sum(values * values, axis=-1, keepdims=True) * (1.0 / count)
    return values * lax.rsqrt(mean + epsilon) * gain_row


def silu_gate(values):
    return values * jax.nn.sigmoid(values)


def softplus(values):
    return jnp.log1p(jnp.exp(values))


def ceil8(rows):
    return -(-rows // 8) * 8


def pad_rows(array, rows):
    return jnp.pad(array, ((0, rows - array.shape[0]), (0, 0)))


MESH = pl.DeviceIdType.MESH


def chip_at(place, chips):
    place = place % chips
    late = place // (chips // 2)
    return (1 - late) * 2 * place + late * (2 * (chips - 1 - place) + 1)


def place_of(chip, chips):
    odd = chip % 2
    return (1 - odd) * (chip // 2) + odd * (chips - 1 - chip // 2)


def gather_kernel(cuts, others, *refs):
    count = len(cuts)
    whole = count + others
    ins, singles = refs[:count], refs[count:whole]
    outs, singles_out = refs[whole : whole + count], refs[whole + count : 2 * whole]
    local_sem, send_sem, recv_sem = refs[2 * whole :]
    dp, chip, core = (lax.axis_index(name) for name in ALL)
    chips = lax.axis_size("chip")
    place = place_of(chip, chips)
    ahead, behind = chip_at(place + 1, chips), chip_at(place + chips - 1, chips)
    to_ahead, to_behind = (dp, ahead, core), (dp, behind, core)
    across, beside = (1 - dp, chip, core), (dp, chip, 1 - core)
    sent = []

    def start(source, target, device):
        index = len(sent)
        copy = pltpu.make_async_remote_copy(
            src_ref=source,
            dst_ref=target,
            send_sem=send_sem.at[index],
            recv_sem=recv_sem.at[index],
            device_id=device,
            device_id_type=MESH,
        )
        copy.start()
        sent.append(copy)
        return copy

    kept = [
        pltpu.make_async_copy(ins[t], outs[t].at[dp, chip, core], local_sem.at[t])
        for t in range(count)
    ]
    for copy in kept:
        copy.start()

    barrier = pltpu.get_barrier_semaphore()
    for device in (to_ahead, to_behind, across, beside):
        pl.semaphore_signal(barrier, inc=1, device_id=device, device_id_type=MESH)
    pl.semaphore_wait(barrier, 4)

    def early(t, at):
        return outs[t].at[:, chip_at(at, chips), core, :, pl.ds(0, cuts[t])]

    def late(t, side, at):
        wide = outs[t].shape[-1] - cuts[t]
        return outs[t].at[side, chip_at(at, chips), core, :, pl.ds(cuts[t], wide)]

    def forward(t, at):
        return late(t, dp, at)

    has_late = [t for t in range(count) if outs[t].shape[-1] > cuts[t]]
    crossing = []
    for t in range(count):
        columns = pl.ds(0, cuts[t])
        crossing.append(
            start(ins[t].at[:, columns], outs[t].at[dp, chip, core, :, columns], across)
        )
    for copy in kept:
        copy.wait()

    longer, shorter = chips // 2, (chips - 1) // 2
    hops_late = [(shorter, longer) if t % 2 == 0 else (longer, shorter) for t in range(count)]
    hops_early = [(longer, shorter) if t % 2 == 0 else (shorter, longer) for t in range(count)]
    landed = []
    crossed = []

    def pass_late(t, at):
        crossed.append((t, at, start(forward(t, at), forward(t, at), across)))
        landed.append(start(forward(t, at), forward(t, at), beside))

    rings = []
    for t in has_late:
        up = start(forward(t, place), forward(t, place), to_ahead)
        down = start(forward(t, place), forward(t, place), to_behind)
        pass_late(t, place)
        rings.append([t, up, down])
    landed += [start(one, two, across) for one, two in zip(singles, singles_out)]
    early_rings = []
    for t in range(count):
        crossing[t].wait_recv()
        up = start(early(t, place), early(t, place), to_ahead)
        down = start(early(t, place), early(t, place), to_behind)
        landed.append(start(early(t, place), early(t, place), beside))
        early_rings.append([t, up, down])
    for hop in range(1, chips // 2 + 1):
        above, below = place + chips - hop, place + hop
        for ring in rings:
            t, up, down = ring
            up_late, down_late = hops_late[t]
            if hop <= up_late:
                up.wait_recv()
                if hop < up_late:
                    ring[1] = start(forward(t, above), forward(t, above), to_ahead)
                pass_late(t, above)
            if hop <= down_late:
                down.wait_recv()
                if hop < down_late:
                    ring[2] = start(forward(t, below), forward(t, below), to_behind)
                pass_late(t, below)
        for ring in early_rings:
            t, up, down = ring
            up_early, down_early = hops_early[t]
            if hop <= up_early:
                up.wait_recv()
                if hop < up_early:
                    ring[1] = start(early(t, above), early(t, above), to_ahead)
                landed.append(start(early(t, above), early(t, above), beside))
            if hop <= down_early:
                down.wait_recv()
                if hop < down_early:
                    ring[2] = start(early(t, below), early(t, below), to_behind)
                landed.append(start(early(t, below), early(t, below), beside))
    for t, at, copy in crossed:
        copy.wait_recv()
        landed.append(start(late(t, 1 - dp, at), late(t, 1 - dp, at), beside))
    for copy in landed:
        copy.wait_recv()
    for copy in sent:
        copy.wait_send()


def gather_everywhere(shards_of, cuts, others):
    chips = lax.axis_size("chip")
    slots = len(others)
    for part, cut in zip(shards_of, cuts):
        slots += 2 * chips + (4 * chips - 1 if part.shape[1] > cut else 0)
    arrays = list(shards_of) + list(others)
    outs = [jax.ShapeDtypeStruct((2, chips, 2) + part.shape, part.dtype) for part in shards_of]
    outs += [jax.ShapeDtypeStruct(part.shape, part.dtype) for part in others]
    moved = sum(4 * chips * part.size * 2 for part in shards_of)
    return pl.pallas_call(
        functools.partial(gather_kernel, cuts, len(others)),
        in_specs=[pl.BlockSpec(memory_space=pl.ANY)] * len(arrays),
        out_specs=[pl.BlockSpec(memory_space=pl.ANY)] * len(arrays),
        out_shape=outs,
        scratch_shapes=[
            pltpu.SemaphoreType.DMA((len(shards_of),)),
            pltpu.SemaphoreType.DMA((slots,)),
            pltpu.SemaphoreType.DMA((slots,)),
        ],
        compiler_params=pltpu.CompilerParams(collective_id=0, has_side_effects=True),
        cost_estimate=pl.CostEstimate(flops=0, bytes_accessed=6 * moved, transcendentals=0),
        name="gather_everywhere",
    )(*arrays)


def ring_kernel(cuts, *refs):
    count = len(cuts)
    ins, outs = refs[:count], refs[count : 2 * count]
    slots = [refs[2 * count + 2 * t : 2 * count + 2 * t + 2] for t in range(count)]
    send_sem, recv_sem = refs[4 * count :]
    dp, chip, core = (lax.axis_index(name) for name in ALL)
    chips = lax.axis_size("chip")
    place = place_of(chip, chips)
    ahead, behind = chip_at(place + 1, chips), chip_at(place + chips - 1, chips)
    devices = ((dp, ahead, core), (dp, behind, core))

    barrier = pltpu.get_barrier_semaphore()
    for device in devices:
        pl.semaphore_signal(barrier, inc=1, device_id=device, device_id_type=MESH)
    pl.semaphore_wait(barrier, 2)

    def columns(t, way):
        return pl.ds(0, cuts[t]) if way == 0 else pl.ds(cuts[t], ins[t].shape[-1] - cuts[t])

    def block(t, way, step):
        at = place + 2 * chips - 2 - step if way == 0 else place + 2 + step
        return ins[t].at[chip_at(at, chips), :, columns(t, way)]

    def copy(t, way, step, source):
        return pltpu.make_async_remote_copy(
            src_ref=source,
            dst_ref=slots[t][way].at[step],
            send_sem=send_sem.at[t, way, step],
            recv_sem=recv_sem.at[t, way, step],
            device_id=devices[way],
            device_id_type=MESH,
        )

    pairs = [(t, way) for t in range(count) for way in (0, 1)]
    for t, way in pairs:
        copy(t, way, 0, block(t, way, -1)).start()

    def hop(step, carry):
        for t, way in pairs:
            slot = slots[t][way].at[step - 1]
            copy(t, way, step - 1, slot).wait_recv()
            own = block(t, way, step - 1)[...].astype(jnp.float32)
            slot[...] = (slot[...].astype(jnp.float32) + own).astype(jnp.bfloat16)
            copy(t, way, step, slot).start()
        return carry

    lax.fori_loop(1, chips - 1, hop, 0)
    last = chips - 2
    for t, way in pairs:
        slot = slots[t][way].at[last]
        copy(t, way, last, slot).wait_recv()
        total = slot[...].astype(jnp.float32) + block(t, way, last)[...].astype(jnp.float32)
        outs[t][:, columns(t, way)] = total.astype(outs[t].dtype)

    def finish(step, carry):
        for t, way in pairs:
            copy(t, way, step, slots[t][way].at[step]).wait_send()
        return carry

    lax.fori_loop(0, chips - 1, finish, 0)


def ring_scatter(totals):
    chips = lax.axis_size("chip")
    cuts = [-(-total.shape[2] // (2 * LANES)) * LANES for total in totals]
    vmem = pl.BlockSpec(memory_space=pltpu.VMEM)
    slots = []
    for total, cut in zip(totals, cuts):
        for width in (cut, total.shape[2] - cut):
            slots.append(pltpu.VMEM((chips - 1, total.shape[1], width), jnp.bfloat16))
    return pl.pallas_call(
        functools.partial(ring_kernel, cuts),
        in_specs=[vmem] * len(totals),
        out_specs=[vmem] * len(totals),
        out_shape=[jax.ShapeDtypeStruct(total.shape[1:], jnp.float32) for total in totals],
        scratch_shapes=slots
        + [
            pltpu.SemaphoreType.DMA((len(totals), 2, chips - 1)),
            pltpu.SemaphoreType.DMA((len(totals), 2, chips - 1)),
        ],
        compiler_params=pltpu.CompilerParams(
            collective_id=1, has_side_effects=True, vmem_limit_bytes=VMEM_LIMIT
        ),
        cost_estimate=pl.CostEstimate(
            flops=0, bytes_accessed=sum(8 * total.size for total in totals), transcendentals=0
        ),
        name="ring_scatter",
    )(*totals)


def meet(one, two, bit, send):
    kept, given = jnp.where(bit == 0, one, two), jnp.where(bit == 0, two, one)
    return kept.astype(jnp.float32) + send(given).astype(jnp.float32)


def halve_dp(total):
    columns = total.shape[-1] // 2
    return meet(total[..., :columns], total[..., columns:], lax.axis_index("dp"), swap)


def split_lanes(array):
    half = array.shape[1] // 2
    return jnp.concatenate([pad_lanes(array[:, :half]), pad_lanes(array[:, half:])], axis=1)


def pad_lanes(array):
    columns = array.shape[1]
    return jnp.pad(array, ((0, 0), (0, -columns % LANES)))


def repack_kernel(count, source, target, start, keep, in_ref, out_ref):
    rows = in_ref.shape[0]
    pieces = []
    for block in range(count):
        at = block * source + start
        pieces.append(in_ref[:, at : at + keep].astype(jnp.float32))
        if target > keep:
            pieces.append(jnp.zeros((rows, target - keep), jnp.float32))
    out_ref[...] = jnp.concatenate(pieces, axis=1).astype(out_ref.dtype)


def repack(array, count, source, target, start=0, keep=None):
    keep = min(source, target) if keep is None else keep
    rows = array.shape[0]
    if source == target and keep == source:
        return array
    step = 64 if rows % 64 == 0 else rows
    return pl.pallas_call(
        functools.partial(repack_kernel, count, source, target, start, keep),
        grid=(rows // step,),
        in_specs=[pl.BlockSpec((step, count * source), lambda r: (r, 0))],
        out_specs=pl.BlockSpec((step, count * target), lambda r: (r, 0)),
        out_shape=jax.ShapeDtypeStruct((rows, count * target), array.dtype),
        compiler_params=params(),
        name="repack",
    )(array)


def weave_kernel(count, source, keep, one_ref, two_ref, out_ref):
    pieces = []
    for block in range(count):
        for ref in (one_ref, two_ref):
            pieces.append(ref[:, block * source : block * source + keep].astype(jnp.float32))
    out_ref[...] = jnp.concatenate(pieces, axis=1)


def weave(one, two, count, source, keep):
    rows = one.shape[0]
    return pl.pallas_call(
        functools.partial(weave_kernel, count, source, keep),
        out_shape=jax.ShapeDtypeStruct((rows, 2 * count * keep), jnp.float32),
        compiler_params=pltpu.CompilerParams(vmem_limit_bytes=VMEM_LIMIT),
        name="weave",
    )(one, two)


def convolve(extended, kernel, bias_row):
    length = extended.shape[0] - kernel.shape[1] + 1
    convolved = bias_row
    for offset in range(kernel.shape[1]):
        convolved = convolved + kernel[:, offset] * extended[offset : offset + length, :]
    return convolved


def decay_rates(decay_wide):
    return -jnp.exp(decay_wide.T)


def gating(scanned, gate_path):
    return scanned * silu_gate(gate_path)


def activate(gate_pre, up_pre):
    return silu_gate(gate_pre) * up_pre


def dot(left, right):
    return jnp.dot(left, right, preferred_element_type=jnp.float32)


def dot_rows(left, right):
    return lax.dot_general(left, right, (((0,), (0,)), ((), ())), preferred_element_type=jnp.float32)


def dot_columns(left, right):
    return lax.dot_general(left, right, (((1,), (1,)), ((), ())), preferred_element_type=jnp.float32)


def combine_paths(attended, mamba_path, attention_row, mamba_row):
    return jnp.concatenate(
        [
            rms_norm(attended, attention_row, attended.shape[-1]),
            rms_norm(mamba_path, mamba_row, mamba_path.shape[-1]),
        ],
        axis=-1,
    )


def shards(
    tokens,
    cotangent,
    input_gain,
    merged_weight,
    meta_tokens,
    select_weight,
    step_weight,
    decay_log,
    conv_weight,
    conv_bias,
    step_bias,
    skip_gain,
    attention_gain,
    mamba_gain,
    output_weight,
    second_gain,
    expand_weight,
    down_weight,
):
    parts = lax.axis_size("chip") * lax.axis_size("core")
    position = lax.axis_index(SEQ)
    first = lax.axis_index("dp") == 0
    tokens = tokens[0]
    cotangent = cotangent[0]
    local_len, width = tokens.shape
    query_width = HEADS * HEAD
    key_width = KVHEADS * HEAD
    inner_start = query_width + 2 * key_width
    half = merged_weight.shape[1]
    reach_count = (WINDOW - 1) // local_len + 1
    rows_in = merged_weight.shape[0]
    rows_pad = ceil8(rows_in)
    rows_channel = select_weight.shape[0]
    channel_pad = ceil8(rows_channel)
    rows_joined = output_weight.shape[0]
    joined_pad = ceil8(rows_joined)
    rows_hidden = down_weight.shape[0]
    hidden_half = rows_hidden // 2
    hidden_pad = ceil8(hidden_half)
    hidden_width = parts * hidden_pad
    wide = lambda row: row.astype(jnp.float32)
    conv_bias_wide = wide(conv_bias)
    step_bias_wide = wide(step_bias)
    skip_wide = wide(skip_gain)[None]
    input_row, second_row = wide(input_gain), wide(second_gain)
    attention_row, mamba_row = wide(attention_gain), wide(mamba_gain)

    columns = [weight.shape[1] for weight in (select_weight, step_weight, decay_log, conv_weight)]
    small = jnp.concatenate([select_weight, step_weight, decay_log, conv_weight], axis=1)
    small = jnp.pad(small, ((0, channel_pad - rows_channel), (0, LANES - sum(columns))))
    meta_part = jnp.pad(
        meta_tokens, ((0, rows_pad - rows_in), (0, LANES - meta_tokens.shape[1]))
    )
    small = jnp.concatenate([small, meta_part], axis=0)
    expand_rows = pad_rows(expand_weight, rows_pad)
    expand_halves = [
        repack(expand_rows, parts, rows_hidden, hidden_pad, at, hidden_half)
        for at in (0, hidden_half)
    ]
    down_halves = [
        pad_rows(down_weight[:hidden_half], hidden_pad),
        pad_rows(down_weight[hidden_half:], hidden_pad),
    ]
    cut = output_weight.shape[1]
    merged_full, output_full, small_full, expand_got, down_got, cotangent_got = gather_everywhere(
        [
            pad_lanes(pad_rows(merged_weight, rows_pad)),
            pad_lanes(pad_rows(output_weight, joined_pad)),
            small,
        ],
        (17 * LANES, 4 * LANES, LANES),
        [
            jnp.where(first, expand_halves[1], expand_halves[0]),
            jnp.where(first, down_halves[1], down_halves[0]),
            cotangent,
        ],
    )
    merged_full = merged_full.reshape(2, parts * rows_pad, -1)
    output_full = output_full.reshape(2, parts * joined_pad, -1)
    small_full = small_full.reshape(2, parts, channel_pad + rows_pad, LANES)
    kept = jnp.where(first, expand_halves[0], expand_halves[1])
    expand_mine = jnp.concatenate(
        [jnp.where(first, kept, expand_got), jnp.where(first, expand_got, kept)], axis=1
    )
    kept = jnp.where(first, down_halves[0], down_halves[1])
    down_mine = jnp.concatenate(
        [jnp.where(first, kept, down_got), jnp.where(first, down_got, kept)], axis=1
    )
    small_full, merged_full, expand_mine, down_mine = lax.optimization_barrier(
        (small_full, merged_full, expand_mine, down_mine)
    )
    expand_full = lax.all_gather(expand_mine, SEQ).reshape(parts * rows_pad, 2 * hidden_width)
    down_full = lax.all_gather(down_mine, SEQ).reshape(hidden_width, width)
    cotangent_both = jnp.concatenate([cotangent, cotangent_got], axis=0)
    channel_rows = [part[:, :rows_channel].reshape(MINNER, LANES) for part in small_full]
    pieces, at = [], 0
    for count in columns:
        pieces.append(jnp.concatenate([channel_rows[h][:, at : at + count] for h in (0, 1)], axis=1))
        at += count
    select_full, step_full, decay_full, kernel_full = pieces
    meta_full = jnp.concatenate(
        [
            small_full[h][:, channel_pad:, : meta_tokens.shape[1]].reshape(
                parts * rows_pad, meta_tokens.shape[1]
            )
            for h in (0, 1)
        ],
        axis=1,
    )

    tokens_wide = wide(tokens)
    normed_wide, norm_back = jax.vjp(lambda v, g: rms_norm(v, g, width), tokens_wide, input_row)
    normed = repack(normed_wide.astype(jnp.bfloat16), parts, rows_in, rows_pad)
    input_row_pad = jnp.pad(
        input_row.reshape(parts, rows_in), ((0, 0), (0, rows_pad - rows_in))
    ).reshape(parts * rows_pad)
    meta_wide, meta_back = jax.vjp(
        lambda v, g: rms_norm(v, g, width), wide(meta_full).T, input_row_pad
    )
    stacked_normed = jnp.concatenate([normed, meta_wide.astype(jnp.bfloat16)], axis=0)
    projected_one = dot(stacked_normed, merged_full[0])
    projected_two = dot(normed, merged_full[1])
    queries = projected_one[:local_len, :query_width].astype(jnp.bfloat16)
    pairs_own = projected_one[:local_len, query_width:inner_start].astype(jnp.bfloat16)
    meta_pairs = projected_one[local_len:, query_width:inner_start].astype(jnp.bfloat16)
    inner_path = jnp.concatenate(
        [
            projected_one[:local_len, inner_start:half].astype(jnp.bfloat16),
            projected_two[:, : inner_start + MINNER - half].astype(jnp.bfloat16),
        ],
        axis=1,
    )
    gate_path = projected_two[:, inner_start + MINNER - half : half]

    pairs = jnp.concatenate(
        [meta_pairs]
        + [from_behind(pairs_own, behind) for behind in range(reach_count, 0, -1)]
        + [pairs_own],
        axis=0,
    )
    where = jnp.reshape(position, (1,)).astype(jnp.int32)
    heads_first = lambda rows: jnp.moveaxis(rows.reshape(rows.shape[0], KVHEADS, HEAD), 1, 0)
    keys, values = heads_first(pairs[:, :key_width]), heads_first(pairs[:, key_width:])
    key_turned, value_turned = pairs[:, :key_width].T, pairs[:, key_width:].T
    query_turned = queries.T
    attended_turned, logs = attend(where, query_turned, keys, value_turned, reach_count + 1)
    attended = attended_turned.T

    previous = from_behind(inner_path[local_len - (CONV - 1) :], 1)
    extended = wide(jnp.concatenate([previous, inner_path], axis=0))
    kernel = wide(kernel_full)
    convolved, convolve_back = jax.vjp(convolve, extended, kernel, conv_bias_wide)
    activated, silu_back = jax.vjp(silu_gate, convolved)
    signal = activated.astype(jnp.bfloat16)
    selected = dot(signal, select_full)
    step_raw = selected[:, :DTR].astype(jnp.bfloat16)
    spread_lanes = lambda mix: jnp.broadcast_to(mix[:, :, None], (local_len, STATE, LANES))
    write_wide = spread_lanes(selected[:, DTR : DTR + STATE])
    read_wide = spread_lanes(selected[:, DTR + STATE :])
    step_pre = dot_columns(step_raw, step_full) + step_bias_wide
    step_size = softplus(step_pre)
    decays, decay_back = jax.vjp(decay_rates, wide(decay_full))
    ends = scan_ends(step_size, signal, write_wide, decays)
    ends, expand_full = lax.optimization_barrier((ends, expand_full))
    total = jnp.sum(step_size, axis=0, keepdims=True)
    coarse = lax.reduce_precision(total, 8, 7)
    carried = lax.all_gather(
        jnp.concatenate([ends, coarse, total - coarse], axis=0).astype(jnp.bfloat16), SEQ
    )
    totals = wide(carried[:, STATE : STATE + 1]) + wide(carried[:, STATE + 1 :])
    scanned, enter = scan_forward(
        where, step_size, signal, write_wide, read_wide, decays, skip_wide, totals, carried[:, :STATE]
    )
    mamba_path, gating_back = jax.vjp(gating, scanned, gate_path)
    joined_wide, paths_back = jax.vjp(
        combine_paths, attended, mamba_path, attention_row, mamba_row
    )
    joined = repack(joined_wide.astype(jnp.bfloat16), parts, rows_joined, joined_pad)
    hidden = tokens_wide + 0.5 * jnp.concatenate(
        [dot(joined, output_full[0])[:, :cut], dot(joined, output_full[1])[:, :cut]], axis=1
    )

    normed_two_wide, norm_two_back = jax.vjp(lambda v, g: rms_norm(v, g, width), hidden, second_row)
    normed_two = repack(normed_two_wide.astype(jnp.bfloat16), parts, rows_in, rows_pad)
    normed_both = jnp.concatenate([normed_two, swap(normed_two)], axis=0)
    expanded = dot(normed_both, expand_full)
    active_wide, activate_back = jax.vjp(
        activate, expanded[:, :hidden_width], expanded[:, hidden_width:]
    )
    active = active_wide.astype(jnp.bfloat16)
    down_out = dot(active, down_full)
    block_output = (
        hidden + down_out[:local_len] + wide(swap(down_out[local_len:].astype(jnp.bfloat16)))
    ).astype(jnp.bfloat16)

    hidden_columns = parity_columns(active, parts, hidden_pad)
    down_grad = grad_parts(hidden_columns, pad_lanes(cotangent_both))
    down_sum = scatter_rows(down_grad, hidden_pad)
    active_grad = dot_columns(cotangent_both, down_full)
    gate_grad, up_grad = activate_back(active_grad)
    expand_in = jnp.concatenate(
        [gate_grad.astype(jnp.bfloat16), up_grad.astype(jnp.bfloat16)], axis=1
    )
    expand_in, block_output = lax.optimization_barrier((expand_in, block_output))
    second_both = dot_columns(expand_in, expand_full)
    second_normed_grad = repack(
        second_both[:local_len] + wide(swap(second_both[local_len:].astype(jnp.bfloat16))),
        parts,
        rows_pad,
        rows_in,
    )
    hidden_part, second_gain_grad = norm_two_back(second_normed_grad)
    hidden_grad = hidden_part + wide(cotangent)
    mixed_in = hidden_grad.astype(jnp.bfloat16)
    mixed_split = split_lanes(mixed_in)
    cut_pad = mixed_split.shape[1] // 2
    joined_grad = repack(
        0.5
        * (
            dot_columns(mixed_split[:, :cut_pad], output_full[0])
            + dot_columns(mixed_split[:, cut_pad:], output_full[1])
        ),
        parts,
        joined_pad,
        rows_joined,
    )
    attended_grad, mamba_grad, attention_gain_grad, mamba_gain_grad = paths_back(joined_grad)
    scanned_grad, gate_path_grad = gating_back(mamba_grad)
    own_pull = scan_pulls(step_size, scanned_grad, read_wide, decays).astype(jnp.bfloat16)
    pulls = lax.all_gather(own_pull, SEQ)

    normed_both, joined, own_pull, down_sum = lax.optimization_barrier(
        (normed_both, joined, own_pull, down_sum)
    )
    both_split = parity_columns(normed_both, parts, rows_pad)
    gate_total = grad_parts(both_split, expand_in[:, :hidden_width])
    up_total = grad_parts(both_split, expand_in[:, hidden_width:])
    output_grad = grad_parts(parity_columns(joined, parts, joined_pad), mixed_split, 0.5)
    kept = jnp.where(first, down_sum[:, :cut], down_sum[:, cut : 2 * cut])
    got = swap(jnp.where(first, down_sum[:, cut : 2 * cut], down_sum[:, :cut]))
    down_out_grad = jnp.concatenate(
        [
            jnp.where(first, kept, got)[:hidden_half],
            jnp.where(first, got, kept)[:hidden_half],
        ],
        axis=0,
    )
    attended_in, gate_total, up_total, output_grad, pulls, down_out_grad = lax.optimization_barrier(
        (attended_grad.astype(jnp.bfloat16), gate_total, up_total, output_grad, pulls, down_out_grad)
    )
    gate_sum = scatter_rows(gate_total, rows_pad)
    up_sum = scatter_rows(up_total, rows_pad)
    output_grad = halve_dp(output_grad).astype(jnp.bfloat16)

    query_grad_turned, key_grads, value_grads = attend_back(
        where,
        query_turned,
        attended_in.T,
        attended_turned,
        logs,
        keys,
        values,
        key_turned,
        reach_count + 1,
    )
    heads_last = lambda grads: jnp.moveaxis(grads, 0, 1).reshape(grads.shape[1], key_width)
    pair_grads = jnp.concatenate([heads_last(key_grads), heads_last(value_grads)], axis=1)
    meta_pair_grad, window_grad = pair_grads[:META], pair_grads[META:]
    own_grad = window_grad[reach_count * local_len :]
    for behind in range(1, reach_count + 1):
        own_grad = own_grad + wide(
            from_behind(
                window_grad[
                    (reach_count - behind) * local_len : (reach_count - behind + 1) * local_len
                ].astype(jnp.bfloat16),
                -behind,
            )
        )

    own_grad, meta_pair_grad, gate_sum, output_grad = lax.optimization_barrier(
        (own_grad, meta_pair_grad, gate_sum, output_grad)
    )
    output_sum = scatter_rows(output_grad, joined_pad)
    with_meta = lambda rows, meta: jnp.concatenate([rows, meta], axis=0)
    query_in = with_meta(query_grad_turned.T, jnp.zeros((META, query_width), jnp.bfloat16))
    pair_in = with_meta(own_grad, meta_pair_grad).astype(jnp.bfloat16)
    gate_in = with_meta(gate_path_grad.astype(jnp.bfloat16), jnp.zeros((META, MINNER), jnp.bfloat16))
    normed_split = parity_columns(stacked_normed, parts, rows_pad)
    early_grad = grad_parts(
        normed_split, pad_lanes(jnp.concatenate([gate_in, query_in, pair_in], axis=1))
    )
    scanned_grad, early_grad = lax.optimization_barrier((scanned_grad, early_grad))
    signal_grad, step_grad, write_parts, read_parts, decays_grad, skip_parts = scan_backward(
        where,
        step_size,
        signal,
        scanned_grad,
        write_wide,
        read_wide,
        decays,
        skip_wide,
        enter,
        totals,
        pulls,
    )
    step_grad, up_sum = lax.optimization_barrier((step_grad, up_sum))
    step_pre_grad = step_grad * jax.nn.sigmoid(step_pre)
    step_in = step_pre_grad.astype(jnp.bfloat16)
    step_weight_grad = dot_rows(step_in, step_raw)
    selected_in = jnp.concatenate(
        [dot(step_in, step_full), jnp.sum(write_parts, axis=-1), jnp.sum(read_parts, axis=-1)],
        axis=-1,
    ).astype(jnp.bfloat16)
    select_grad = dot_rows(signal, selected_in)
    signal_grad = signal_grad + dot_columns(selected_in, select_full)
    extended_grad, kernel_grad, conv_bias_grad = convolve_back(silu_back(signal_grad)[0])
    returned_tail = wide(from_behind(extended_grad[: CONV - 1].astype(jnp.bfloat16), -1))
    inner_grad = extended_grad[CONV - 1 :] + jnp.pad(
        returned_tail, ((local_len - (CONV - 1), 0), (0, 0))
    )
    decay_grad = decay_back(decays_grad)[0]

    inner_in = with_meta(inner_grad.astype(jnp.bfloat16), jnp.zeros((META, MINNER), jnp.bfloat16))
    inner_in, output_sum = lax.optimization_barrier((inner_in, output_sum))
    inner_cut = half - inner_start
    inner_first = -(-inner_cut // LANES) * LANES
    inner_grads = grad_parts(
        normed_split,
        jnp.concatenate([pad_lanes(inner_in[:, :inner_cut]), pad_lanes(inner_in[:, inner_cut:])], axis=1),
    )
    one_in = pad_lanes(jnp.concatenate([query_in, pair_in, inner_in[:, :inner_cut]], axis=1))
    two_in = pad_lanes(
        jnp.concatenate([inner_in[:local_len, inner_cut:], gate_in[:local_len]], axis=1)
    )
    stacked_grad = dot_columns(one_in, merged_full[0])
    normed_grad = repack(
        stacked_grad[:local_len] + dot_columns(two_in, merged_full[1]), parts, rows_pad, rows_in
    )
    meta_rows_grad, meta_gain_grad = meta_back(stacked_grad[local_len:])
    tokens_part, input_gain_part = norm_back(normed_grad)
    tokens_grad = hidden_grad + tokens_part
    input_gain_grad = input_gain_part + (
        meta_gain_grad.reshape(parts, rows_pad)[:, :rows_in].reshape(width)
    )

    count = meta_tokens.shape[1]
    meta_grads = jnp.pad(
        meta_rows_grad.T.reshape(parts, rows_pad, META),
        ((0, 0), (0, channel_pad - rows_pad), (0, 0)),
    )
    sides = []
    for h in (0, 1):
        cuts = [
            grad[:, h * size : (h + 1) * size]
            for grad, size in zip((select_grad, step_weight_grad, decay_grad, kernel_grad), columns)
        ]
        side = jnp.concatenate(cuts, axis=1).reshape(parts, rows_channel, sum(columns))
        side = jnp.pad(
            side, ((0, 0), (0, channel_pad - rows_channel), (0, LANES - sum(columns)))
        )
        meta_side = meta_grads[:, :, h * count : (h + 1) * count]
        sides += [side, jnp.pad(meta_side, ((0, 0), (0, 0), (0, LANES - count)))]
    small_grads = jnp.concatenate(sides, axis=2).astype(jnp.bfloat16)
    small_grads = small_grads.reshape(parts // 2, 2, channel_pad, 4 * LANES)
    small_sum = meet(
        small_grads[:, 0],
        small_grads[:, 1],
        lax.axis_index("core"),
        lambda array: swap(array, "core"),
    )
    inner_sum, early_out, small_sum = ring_scatter(
        [
            inner_grads.reshape(parts // 2, rows_pad, -1),
            early_grad.reshape(parts // 2, rows_pad, -1),
            small_sum.astype(jnp.bfloat16),
        ]
    )
    output_out = wide(output_sum)[:rows_joined, :cut]
    pair_early = jnp.pad(
        early_out[:, MINNER : MINNER + inner_start], ((0, 0), (0, MINNER - inner_start))
    )
    early_out = meet(
        pair_early,
        early_out[:, :MINNER],
        lax.axis_index("dp"),
        lambda array: swap(array.astype(jnp.bfloat16)),
    )[:rows_in]
    small_sum = halve_dp(small_sum)
    inner_one, inner_two = inner_sum[:, :inner_first], inner_sum[:, inner_first:]
    inner_two = jnp.pad(inner_two, ((0, 0), (0, inner_first - inner_two.shape[1])))
    inner_out = meet(
        inner_one, inner_two, lax.axis_index("dp"), lambda array: swap(array.astype(jnp.bfloat16))
    )[:rows_in]
    small_outs, at = [], 0
    for size in columns:
        small_outs.append(small_sum[:rows_channel, at : at + size])
        at += size
    meta_sum = small_sum[:rows_in, LANES : LANES + count]

    vectors = (
        second_gain_grad,
        attention_gain_grad,
        mamba_gain_grad,
        jnp.sum(skip_parts, axis=0),
        jnp.sum(step_pre_grad, axis=0),
        conv_bias_grad,
        input_gain_grad,
    )
    flat = jnp.concatenate(vectors)
    padded = -(-flat.shape[0] // (8 * LANES)) * 8 * LANES
    flat = sum_everywhere(jnp.pad(flat, (0, padded - flat.shape[0])).reshape(-1, LANES))
    flat = flat.reshape(-1)
    sums, at = [], 0
    for vector in vectors:
        sums.append(flat[at : at + vector.shape[0]])
        at += vector.shape[0]

    rest = half - MINNER
    merged_out = jnp.where(
        first,
        jnp.concatenate([early_out[:, :inner_start], inner_out[:, :inner_cut]], axis=1),
        jnp.concatenate([inner_out[:, :rest], early_out], axis=1),
    )
    gate_part, up_part = gate_sum, up_sum
    kept = jnp.where(first, gate_part, up_part)
    got = swap(jnp.where(first, up_part, gate_part))
    expand_out = weave(
        jnp.where(first, kept, got), jnp.where(first, got, kept), parts, hidden_pad, hidden_half
    )[:rows_in]
    return (
        block_output[None],
        tokens_grad[None],
        sums[6],
        merged_out,
        meta_sum,
        small_outs[0],
        small_outs[1],
        small_outs[2],
        small_outs[3],
        sums[5],
        sums[4],
        sums[3],
        sums[1],
        sums[2],
        output_out,
        sums[0],
        expand_out,
        wide(down_out_grad),
    )


def solution(mesh):
    split = Mesh(mesh.devices.reshape(2, -1, 2), ALL)
    rows, matrix, copied = P("dp", SEQ, None), P(SEQ, "dp"), P()
    return jax.shard_map(
        shards,
        mesh=split,
        in_specs=(rows, rows, copied) + (matrix,) * 6 + (copied,) * 5 + (matrix, copied, matrix, matrix),
        out_specs=(rows, rows, copied) + (matrix,) * 6 + (copied,) * 5 + (matrix, copied, matrix, matrix),
        check_vma=False,
    )
```

```python
import functools

import jax
import jax.numpy as jnp
from jax import lax
from jax.experimental import pallas as pl
from jax.experimental.pallas import tpu as pltpu
from jax.sharding import Mesh
from jax.sharding import PartitionSpec as P

HEADS = 25
KVHEADS = 5
HEAD = 64
MINNER = 3200
STATE = 16
DTR = 100
META = 128
WINDOW = 1024
CONV = 4
epsilon = 1e-06
LANES = 128
STEPS = 8
LOG2E = 1.4426950408889634
VMEM_LIMIT = 60 * 1024 * 1024


def lane_tiles(width):
    return [slice(at, min(at + LANES, width)) for at in range(0, width, LANES)]


def chunk_of(channels):
    for tiles in (5, 4, 6, 3, 2, 7, 1):
        if channels % (tiles * LANES) == 0:
            return tiles * LANES
    return channels


def fold(rows):
    sub = lax.broadcasted_iota(jnp.int32, rows[0].shape, 0)
    for bit in (1, 2, 4):
        clear = (sub & bit) == 0
        rows = [
            jnp.where(clear, one, two) + pltpu.roll(jnp.where(clear, two, one), bit, 0)
            for one, two in zip(rows[0::2], rows[1::2])
        ]
    return rows[0]


def halves(product):
    return product[:8] + product[8:]


def ends_kernel(step_ref, signal_ref, write_ref, decay_ref, end_ref):
    length, width = step_ref.shape
    tiles = lane_tiles(width)
    rates = [decay_ref[:, tile] * LOG2E for tile in tiles]

    def block(at, states):
        states = list(states)
        rows = pl.ds(pl.multiple_of(at * STEPS, STEPS), STEPS)
        step = step_ref[rows, :]
        drive = step * signal_ref[rows, :].astype(jnp.float32)
        for i in range(STEPS):
            write = write_ref[at * STEPS + i]
            for j, tile in enumerate(tiles):
                factor = jnp.exp2(step[i : i + 1, tile] * rates[j])
                states[j] = factor * states[j] + drive[i : i + 1, tile] * write[:, : tile.stop - tile.start]
        return tuple(states)

    zero = tuple(jnp.zeros((STATE, tile.stop - tile.start), jnp.float32) for tile in tiles)
    final = lax.fori_loop(0, length // STEPS, block, zero)
    for j, tile in enumerate(tiles):
        end_ref[:, tile] = final[j]


def pull_kernel(step_ref, grad_ref, read_ref, decay_ref, end_ref):
    length, width = step_ref.shape
    tiles = lane_tiles(width)
    rates = [decay_ref[:, tile] * LOG2E for tile in tiles]
    blocks = length // STEPS

    def block(k, states):
        at = blocks - 1 - k
        states = list(states)
        rows = pl.ds(pl.multiple_of(at * STEPS, STEPS), STEPS)
        step = step_ref[rows, :]
        grad = grad_ref[rows, :]
        for i in reversed(range(STEPS)):
            read = read_ref[at * STEPS + i]
            for j, tile in enumerate(tiles):
                factor = jnp.exp2(step[i : i + 1, tile] * rates[j])
                states[j] = factor * (states[j] + grad[i : i + 1, tile] * read[:, : tile.stop - tile.start])
        return tuple(states)

    zero = tuple(jnp.zeros((STATE, tile.stop - tile.start), jnp.float32) for tile in tiles)
    final = lax.fori_loop(0, blocks, block, zero)
    for j, tile in enumerate(tiles):
        end_ref[:, tile] = final[j]


def carry_over(position, count, reverse, rates, totals_ref, ends_ref, tile):
    def step(k, state):
        at = count - 1 - k if reverse else k
        reached = at > position if reverse else at < position
        factor = jnp.exp2(totals_ref[at, :, tile] * rates)
        new = factor * state + ends_ref[at, :, tile].astype(jnp.float32)
        return jnp.where(reached, new, state)

    return lax.fori_loop(0, count, step, jnp.zeros(rates.shape, jnp.float32))


def scan_kernel(
    position_ref, step_ref, signal_ref, write_ref, read_ref, decay_ref, skip_ref,
    totals_ref, ends_ref, out_ref, enter_ref,
):
    length, width = step_ref.shape
    tiles = lane_tiles(width)
    rates = [decay_ref[:, tile] * LOG2E for tile in tiles]
    enter = tuple(
        carry_over(position_ref[0], totals_ref.shape[0], False, rates[j], totals_ref, ends_ref, tile)
        for j, tile in enumerate(tiles)
    )
    for j, tile in enumerate(tiles):
        enter_ref[:, tile] = enter[j]

    def block(at, states):
        states = list(states)
        rows = pl.ds(pl.multiple_of(at * STEPS, STEPS), STEPS)
        step = step_ref[rows, :]
        signal = signal_ref[rows, :].astype(jnp.float32)
        drive = step * signal
        parts = [[] for tile in tiles]
        for i in range(STEPS):
            write = write_ref[at * STEPS + i]
            read = read_ref[at * STEPS + i]
            for j, tile in enumerate(tiles):
                wide = tile.stop - tile.start
                factor = jnp.exp2(step[i : i + 1, tile] * rates[j])
                states[j] = factor * states[j] + drive[i : i + 1, tile] * write[:, :wide]
                parts[j].append(halves(read[:, :wide] * states[j]))
        for j, tile in enumerate(tiles):
            out_ref[rows, tile] = fold(parts[j]) + skip_ref[:, tile] * signal[:, tile]
        return tuple(states)

    lax.fori_loop(0, length // STEPS, block, enter)


def scan_back_kernel(
    position_ref, step_ref, signal_ref, grad_ref, write_ref, read_ref, decay_ref, skip_ref,
    enter_ref, totals_ref, pulls_ref,
    signal_grad_ref, step_grad_ref, write_grad_ref, read_grad_ref, decay_grad_ref, skip_grad_ref,
    states_ref, factors_ref,
):
    length, width = step_ref.shape
    tiles = lane_tiles(width)
    blocks = length // STEPS
    decays = [decay_ref[:, tile] for tile in tiles]

    @pl.when(pl.program_id(0) == 0)
    def _():
        write_grad_ref[...] = jnp.zeros_like(write_grad_ref)
        read_grad_ref[...] = jnp.zeros_like(read_grad_ref)

    rates = [decay * LOG2E for decay in decays]
    states_ref[0] = enter_ref[...]

    def forward(at, states):
        states = list(states)
        rows = pl.ds(pl.multiple_of(at * STEPS, STEPS), STEPS)
        step = step_ref[rows, :]
        drive = step * signal_ref[rows, :].astype(jnp.float32)
        for i in range(STEPS):
            write = write_ref[at * STEPS + i]
            for j, tile in enumerate(tiles):
                factor = jnp.exp2(step[i : i + 1, tile] * rates[j])
                states[j] = factor * states[j] + drive[i : i + 1, tile] * write[:, : tile.stop - tile.start]
                factors_ref[at * STEPS + i, :, tile] = factor
                states_ref[at * STEPS + i + 1, :, tile] = states[j]
        return tuple(states)

    lax.fori_loop(0, blocks, forward, tuple(enter_ref[:, tile] for tile in tiles))

    leaving = tuple(
        carry_over(position_ref[0], totals_ref.shape[0], True, rates[j], totals_ref, pulls_ref, tile)
        for j, tile in enumerate(tiles)
    )
    zero = tuple(jnp.zeros_like(decay) for decay in decays)
    zero_row = tuple(jnp.zeros((STEPS, tile.stop - tile.start), jnp.float32) for tile in tiles)

    def backward(k, carry):
        at = blocks - 1 - k
        adjoint, decay_sum, skip_sum = (list(part) for part in carry)
        rows = pl.ds(pl.multiple_of(at * STEPS, STEPS), STEPS)
        step = step_ref[rows, :]
        signal = signal_ref[rows, :].astype(jnp.float32)
        grad = grad_ref[rows, :]
        drive = step * signal
        by_write = [[None] * STEPS for tile in tiles]
        by_decay = [[None] * STEPS for tile in tiles]
        for i in reversed(range(STEPS)):
            write = write_ref[at * STEPS + i]
            read = read_ref[at * STEPS + i]
            write_sum = None
            read_sum = None
            for j, tile in enumerate(tiles):
                wide = tile.stop - tile.start
                row = grad[i : i + 1, tile]
                whole = adjoint[j] + read[:, :wide] * row
                adjoint[j] = factors_ref[at * STEPS + i, :, tile] * whole
                kept = adjoint[j] * states_ref[at * STEPS + i, :, tile]
                decay_sum[j] = decay_sum[j] + step[i : i + 1, tile] * kept
                by_decay[j][i] = halves(decays[j] * kept)
                by_write[j][i] = halves(write[:, :wide] * whole)
                write_part = drive[i : i + 1, tile] * whole
                read_part = row * states_ref[at * STEPS + i + 1, :, tile]
                write_sum = write_part if write_sum is None else write_sum + write_part
                read_sum = read_part if read_sum is None else read_sum + read_part
            write_grad_ref[at * STEPS + i] += write_sum
            read_grad_ref[at * STEPS + i] += read_sum
        for j, tile in enumerate(tiles):
            written = fold(by_write[j])
            signal_grad_ref[rows, tile] = step[:, tile] * written + skip_ref[:, tile] * grad[:, tile]
            step_grad_ref[rows, tile] = signal[:, tile] * written + fold(by_decay[j])
            skip_sum[j] = skip_sum[j] + grad[:, tile] * signal[:, tile]
        return tuple(adjoint), tuple(decay_sum), tuple(skip_sum)

    carry = lax.fori_loop(0, blocks, backward, (leaving, zero, zero_row))
    for j, tile in enumerate(tiles):
        decay_grad_ref[:, tile] = carry[1][j]
        skip_grad_ref[:, tile] = carry[2][j]


def by_chunk(rows, chunk):
    return pl.BlockSpec((rows, chunk), lambda c: (0, c))


def stacked(count, rows, chunk):
    return pl.BlockSpec((count, rows, chunk), lambda c: (0, 0, c))


def whole(shape):
    return pl.BlockSpec(shape, lambda c: (0,) * len(shape))


def params():
    return pltpu.CompilerParams(vmem_limit_bytes=VMEM_LIMIT, dimension_semantics=("arbitrary",))


def scan_ends(step_size, signal, write_wide, decays):
    length, channels = step_size.shape
    chunk = chunk_of(channels)
    return pl.pallas_call(
        ends_kernel,
        grid=(channels // chunk,),
        in_specs=[by_chunk(length, chunk), by_chunk(length, chunk), whole(write_wide.shape), by_chunk(STATE, chunk)],
        out_specs=by_chunk(STATE, chunk),
        out_shape=jax.ShapeDtypeStruct((STATE, channels), jnp.float32),
        compiler_params=params(),
        name="scan_ends",
    )(step_size, signal, write_wide, decays)


def scan_pulls(step_size, grad, read_wide, decays):
    length, channels = step_size.shape
    chunk = chunk_of(channels)
    return pl.pallas_call(
        pull_kernel,
        grid=(channels // chunk,),
        in_specs=[by_chunk(length, chunk), by_chunk(length, chunk), whole(read_wide.shape), by_chunk(STATE, chunk)],
        out_specs=by_chunk(STATE, chunk),
        out_shape=jax.ShapeDtypeStruct((STATE, channels), jnp.float32),
        compiler_params=params(),
        name="scan_pulls",
    )(step_size, grad, read_wide, decays)


def scan_forward(position, step_size, signal, write_wide, read_wide, decays, skip, totals, ends):
    length, channels = step_size.shape
    chunk = chunk_of(channels)
    parts = totals.shape[0]
    return pl.pallas_call(
        scan_kernel,
        grid=(channels // chunk,),
        in_specs=[
            pl.BlockSpec(memory_space=pltpu.SMEM),
            by_chunk(length, chunk), by_chunk(length, chunk), whole(write_wide.shape), whole(read_wide.shape),
            by_chunk(STATE, chunk), by_chunk(1, chunk), stacked(parts, 1, chunk), stacked(parts, STATE, chunk),
        ],
        out_specs=[by_chunk(length, chunk), by_chunk(STATE, chunk)],
        out_shape=[
            jax.ShapeDtypeStruct((length, channels), jnp.float32),
            jax.ShapeDtypeStruct((STATE, channels), jnp.float32),
        ],
        compiler_params=params(),
        name="scan_forward",
    )(position, step_size, signal, write_wide, read_wide, decays, skip, totals, ends)


def scan_backward(position, step_size, signal, grad, write_wide, read_wide, decays, skip, enter, totals, pulls):
    length, channels = step_size.shape
    chunk = chunk_of(channels)
    parts = totals.shape[0]
    return pl.pallas_call(
        scan_back_kernel,
        grid=(channels // chunk,),
        in_specs=[
            pl.BlockSpec(memory_space=pltpu.SMEM),
            by_chunk(length, chunk), by_chunk(length, chunk), by_chunk(length, chunk),
            whole(write_wide.shape), whole(read_wide.shape),
            by_chunk(STATE, chunk), by_chunk(1, chunk), by_chunk(STATE, chunk), stacked(parts, 1, chunk),
            stacked(parts, STATE, chunk),
        ],
        out_specs=[
            by_chunk(length, chunk), by_chunk(length, chunk), whole(write_wide.shape), whole(read_wide.shape),
            by_chunk(STATE, chunk), by_chunk(STEPS, chunk),
        ],
        out_shape=[
            jax.ShapeDtypeStruct((length, channels), jnp.float32),
            jax.ShapeDtypeStruct((length, channels), jnp.float32),
            jax.ShapeDtypeStruct(write_wide.shape, jnp.float32),
            jax.ShapeDtypeStruct(read_wide.shape, jnp.float32),
            jax.ShapeDtypeStruct((STATE, channels), jnp.float32),
            jax.ShapeDtypeStruct((STEPS, channels), jnp.float32),
        ],
        scratch_shapes=[
            pltpu.VMEM((length + 1, STATE, chunk), jnp.float32),
            pltpu.VMEM((length, STATE, chunk), jnp.float32),
        ],
        compiler_params=params(),
        name="scan_backward",
    )(position, step_size, signal, grad, write_wide, read_wide, decays, skip, enter, totals, pulls)


def key_blocks(keys, span, count):
    meta = keys - count * span
    return [(0, meta, None)] + [(meta + b * span, span, b) for b in range(count)]


def masked(scores, place, count, position, other):
    if place is None:
        return scores
    row = lax.broadcasted_iota(jnp.int32, scores.shape, 0)
    column = lax.broadcasted_iota(jnp.int32, scores.shape, 1)
    if place == count - 1:
        return jnp.where(row <= column, scores, other)
    there = position + place >= count - 1
    if place == 0:
        return jnp.where((row > column) & there, scores, other)
    return jnp.where(there, scores, other)


def attend_kernel(count, position_ref, query_ref, key_ref, value_ref, out_ref, log_ref):
    position = position_ref[0]
    span = query_ref.shape[1]
    group = query_ref.shape[0] // HEAD
    blocks = key_blocks(key_ref.shape[1], span, count)
    for head in range(group):
        rows = slice(head * HEAD, (head + 1) * HEAD)
        query = query_ref[rows, :] * (HEAD**-0.5)
        scores = [
            masked(
                jnp.dot(key_ref[0, at : at + size, :], query, preferred_element_type=jnp.float32),
                place, count, position, -1e30,
            )
            for at, size, place in blocks
        ]
        top = functools.reduce(jnp.maximum, [jnp.max(part, axis=0, keepdims=True) for part in scores])
        powers = [jnp.exp(part - top) for part in scores]
        total = sum(jnp.sum(part, axis=0, keepdims=True) for part in powers)
        out = sum(
            jnp.dot(value_ref[:, at : at + size], part.astype(jnp.bfloat16), preferred_element_type=jnp.float32)
            for (at, size, place), part in zip(blocks, powers)
        )
        out_ref[rows, :] = out / total
        log_ref[0, head : head + 1, :] = top + jnp.log(total)


def attend_back_kernel(
    count, position_ref, query_ref, grad_ref, out_ref, log_ref, key_ref, value_ref, key_turned_ref,
    query_grad_ref, key_grad_ref, value_grad_ref,
):
    position = position_ref[0]
    span = query_ref.shape[1]
    group = query_ref.shape[0] // HEAD
    blocks = key_blocks(key_ref.shape[1], span, count)
    turned = (((1,), (1,)), ((), ()))
    for head in range(group):
        rows = slice(head * HEAD, (head + 1) * HEAD)
        query = query_ref[rows, :] * (HEAD**-0.5)
        grad = grad_ref[rows, :]
        along = jnp.sum(grad.astype(jnp.float32) * out_ref[rows, :], axis=0, keepdims=True)
        log_total = log_ref[0, head : head + 1, :]
        query_sum = jnp.zeros((HEAD, span), jnp.float32)
        for at, size, place in blocks:
            keys = slice(at, at + size)
            score = jnp.dot(key_ref[0, keys, :], query, preferred_element_type=jnp.float32)
            prob = jnp.exp(masked(score, place, count, position, -1e30) - log_total)
            prob_grad = jnp.dot(value_ref[0, keys, :], grad, preferred_element_type=jnp.float32)
            score_grad = (prob * (prob_grad - along)).astype(jnp.bfloat16)
            query_sum += jnp.dot(key_turned_ref[:, keys], score_grad, preferred_element_type=jnp.float32)
            by_key = lax.dot_general(score_grad, query, turned, preferred_element_type=jnp.float32)
            by_value = lax.dot_general(prob.astype(jnp.bfloat16), grad, turned, preferred_element_type=jnp.float32)
            if head == 0:
                key_grad_ref[0, keys, :] = by_key
                value_grad_ref[0, keys, :] = by_value
            else:
                key_grad_ref[0, keys, :] += by_key
                value_grad_ref[0, keys, :] += by_value
        query_grad_ref[rows, :] = (query_sum * (HEAD**-0.5)).astype(query_grad_ref.dtype)


def by_head(rows, columns):
    return pl.BlockSpec((rows, columns), lambda g: (g, 0))


def head_stack(rows, columns):
    return pl.BlockSpec((1, rows, columns), lambda g: (g, 0, 0))


def attend(position, query_turned, keys, value_turned, count):
    span = query_turned.shape[1]
    group = query_turned.shape[0] // KVHEADS
    total = keys.shape[1]
    return pl.pallas_call(
        functools.partial(attend_kernel, count),
        grid=(KVHEADS,),
        in_specs=[
            pl.BlockSpec(memory_space=pltpu.SMEM),
            by_head(group, span), head_stack(total, HEAD), by_head(HEAD, total),
        ],
        out_specs=[by_head(group, span), head_stack(8, span)],
        out_shape=[
            jax.ShapeDtypeStruct(query_turned.shape, jnp.float32),
            jax.ShapeDtypeStruct((KVHEADS, 8, span), jnp.float32),
        ],
        compiler_params=params(),
        name="attend",
    )(position, query_turned, keys, value_turned)


def attend_back(position, query_turned, grad_turned, out_turned, logs, keys, values, key_turned, count):
    span = query_turned.shape[1]
    group = query_turned.shape[0] // KVHEADS
    total = keys.shape[1]
    return pl.pallas_call(
        functools.partial(attend_back_kernel, count),
        grid=(KVHEADS,),
        in_specs=[
            pl.BlockSpec(memory_space=pltpu.SMEM),
            by_head(group, span), by_head(group, span), by_head(group, span), head_stack(8, span),
            head_stack(total, HEAD), head_stack(total, HEAD), by_head(HEAD, total),
        ],
        out_specs=[by_head(group, span), head_stack(total, HEAD), head_stack(total, HEAD)],
        out_shape=[
            jax.ShapeDtypeStruct(query_turned.shape, jnp.bfloat16),
            jax.ShapeDtypeStruct(keys.shape, jnp.float32),
            jax.ShapeDtypeStruct(keys.shape, jnp.float32),
        ],
        compiler_params=params(),
        name="attend_back",
    )(position, query_turned, grad_turned, out_turned, logs, keys, values, key_turned)


SEQ = ("chip", "core")
ALL = ("dp",) + SEQ


def from_behind(array, by):
    size = lax.axis_size("chip") * lax.axis_size("core")
    pairs = [(i, i + by) for i in range(size) if 0 <= i + by < size]
    return lax.ppermute(array, SEQ, pairs)


def swap(array, axis="dp"):
    return lax.ppermute(array, axis, [(0, 1), (1, 0)])


def sum_everywhere(array):
    array = array + swap(array, "core")
    chips = lax.axis_size("chip")
    step = 1
    while step < chips:
        array = array + lax.ppermute(array, "chip", [(i, i ^ step) for i in range(chips)])
        step *= 2
    return array + swap(array)


def parity_kernel(parts, block, core_ref, in_ref, own_ref, other_ref):
    values = in_ref[...].astype(jnp.float32)
    even, odd = [
        jnp.concatenate(
            [values[:, at * block : (at + 1) * block] for at in range(core, parts, 2)], axis=1
        )
        for core in (0, 1)
    ]
    own = core_ref[0] == 0
    own_ref[...] = jnp.where(own, even, odd).astype(own_ref.dtype)
    other_ref[...] = jnp.where(own, odd, even).astype(other_ref.dtype)


def parity_columns(array, parts, block):
    rows = array.shape[0]
    step = 64 if rows % 64 == 0 else rows
    half = pl.BlockSpec((step, parts // 2 * block), lambda r: (r, 0))
    return pl.pallas_call(
        functools.partial(parity_kernel, parts, block),
        grid=(rows // step,),
        in_specs=[
            pl.BlockSpec(memory_space=pltpu.SMEM),
            pl.BlockSpec((step, parts * block), lambda r: (r, 0)),
        ],
        out_specs=[half, half],
        out_shape=[jax.ShapeDtypeStruct((rows, parts // 2 * block), array.dtype)] * 2,
        compiler_params=params(),
        name="parity_columns",
    )(jnp.reshape(lax.axis_index("core"), (1,)).astype(jnp.int32), array)


def grad_parts(left, right, scale=1.0):
    kept, given = left
    sent = (scale * dot_rows(given, right)).astype(jnp.bfloat16)
    got = swap(sent, "core")
    return (scale * dot_rows(kept, right) + got.astype(jnp.float32)).astype(jnp.bfloat16)


def scatter_rows(total, rows):
    chips = lax.axis_size("chip")
    return lax.psum_scatter(total.reshape(chips, rows, -1), "chip", scatter_dimension=0)


def rms_norm(values, gain_row, count):
    mean = jnp.sum(values * values, axis=-1, keepdims=True) * (1.0 / count)
    return values * lax.rsqrt(mean + epsilon) * gain_row


def silu_gate(values):
    return values * jax.nn.sigmoid(values)


def softplus(values):
    return jnp.log1p(jnp.exp(values))


def ceil8(rows):
    return -(-rows // 8) * 8


def pad_rows(array, rows):
    return jnp.pad(array, ((0, rows - array.shape[0]), (0, 0)))


MESH = pl.DeviceIdType.MESH


def chip_at(place, chips):
    place = place % chips
    late = place // (chips // 2)
    return (1 - late) * 2 * place + late * (2 * (chips - 1 - place) + 1)


def place_of(chip, chips):
    odd = chip % 2
    return (1 - odd) * (chip // 2) + odd * (chips - 1 - chip // 2)


def gather_kernel(cuts, others, *refs):
    count = len(cuts)
    whole = count + others
    ins, singles = refs[:count], refs[count:whole]
    outs, singles_out = refs[whole : whole + count], refs[whole + count : 2 * whole]
    local_sem, send_sem, recv_sem = refs[2 * whole :]
    dp, chip, core = (lax.axis_index(name) for name in ALL)
    chips = lax.axis_size("chip")
    place = place_of(chip, chips)
    ahead, behind = chip_at(place + 1, chips), chip_at(place + chips - 1, chips)
    to_ahead, to_behind = (dp, ahead, core), (dp, behind, core)
    across, beside = (1 - dp, chip, core), (dp, chip, 1 - core)
    sent = []

    def start(source, target, device):
        index = len(sent)
        copy = pltpu.make_async_remote_copy(
            src_ref=source,
            dst_ref=target,
            send_sem=send_sem.at[index],
            recv_sem=recv_sem.at[index],
            device_id=device,
            device_id_type=MESH,
        )
        copy.start()
        sent.append(copy)
        return copy

    kept = [
        pltpu.make_async_copy(ins[t], outs[t].at[dp, chip, core], local_sem.at[t])
        for t in range(count)
    ]
    for copy in kept:
        copy.start()

    barrier = pltpu.get_barrier_semaphore()
    for device in (to_ahead, to_behind, across, beside):
        pl.semaphore_signal(barrier, inc=1, device_id=device, device_id_type=MESH)
    pl.semaphore_wait(barrier, 4)

    def early(t, at):
        return outs[t].at[:, chip_at(at, chips), core, :, pl.ds(0, cuts[t])]

    def late(t, side, at):
        wide = outs[t].shape[-1] - cuts[t]
        return outs[t].at[side, chip_at(at, chips), core, :, pl.ds(cuts[t], wide)]

    def forward(t, at):
        return late(t, dp, at)

    has_late = [t for t in range(count) if outs[t].shape[-1] > cuts[t]]
    crossing = []
    for t in range(count):
        columns = pl.ds(0, cuts[t])
        crossing.append(
            start(ins[t].at[:, columns], outs[t].at[dp, chip, core, :, columns], across)
        )
    for copy in kept:
        copy.wait()

    longer, shorter = chips // 2, (chips - 1) // 2
    hops_late = [(shorter, longer) if t % 2 == 0 else (longer, shorter) for t in range(count)]
    hops_early = [(longer, shorter) if t % 2 == 0 else (shorter, longer) for t in range(count)]
    landed = []
    crossed = []

    def pass_late(t, at):
        crossed.append((t, at, start(forward(t, at), forward(t, at), across)))
        landed.append(start(forward(t, at), forward(t, at), beside))

    rings = []
    for t in has_late:
        up = start(forward(t, place), forward(t, place), to_ahead)
        down = start(forward(t, place), forward(t, place), to_behind)
        pass_late(t, place)
        rings.append([t, up, down])
    landed += [start(one, two, across) for one, two in zip(singles, singles_out)]
    early_rings = []
    for t in range(count):
        crossing[t].wait_recv()
        up = start(early(t, place), early(t, place), to_ahead)
        down = start(early(t, place), early(t, place), to_behind)
        landed.append(start(early(t, place), early(t, place), beside))
        early_rings.append([t, up, down])
    for hop in range(1, chips // 2 + 1):
        above, below = place + chips - hop, place + hop
        for ring in rings:
            t, up, down = ring
            up_late, down_late = hops_late[t]
            if hop <= up_late:
                up.wait_recv()
                if hop < up_late:
                    ring[1] = start(forward(t, above), forward(t, above), to_ahead)
                pass_late(t, above)
            if hop <= down_late:
                down.wait_recv()
                if hop < down_late:
                    ring[2] = start(forward(t, below), forward(t, below), to_behind)
                pass_late(t, below)
        for ring in early_rings:
            t, up, down = ring
            up_early, down_early = hops_early[t]
            if hop <= up_early:
                up.wait_recv()
                if hop < up_early:
                    ring[1] = start(early(t, above), early(t, above), to_ahead)
                landed.append(start(early(t, above), early(t, above), beside))
            if hop <= down_early:
                down.wait_recv()
                if hop < down_early:
                    ring[2] = start(early(t, below), early(t, below), to_behind)
                landed.append(start(early(t, below), early(t, below), beside))
    for t, at, copy in crossed:
        copy.wait_recv()
        landed.append(start(late(t, 1 - dp, at), late(t, 1 - dp, at), beside))
    for copy in landed:
        copy.wait_recv()
    for copy in sent:
        copy.wait_send()


def gather_everywhere(shards_of, cuts, others):
    chips = lax.axis_size("chip")
    slots = len(others)
    for part, cut in zip(shards_of, cuts):
        slots += 2 * chips + (4 * chips - 1 if part.shape[1] > cut else 0)
    arrays = list(shards_of) + list(others)
    outs = [jax.ShapeDtypeStruct((2, chips, 2) + part.shape, part.dtype) for part in shards_of]
    outs += [jax.ShapeDtypeStruct(part.shape, part.dtype) for part in others]
    moved = sum(4 * chips * part.size * 2 for part in shards_of)
    return pl.pallas_call(
        functools.partial(gather_kernel, cuts, len(others)),
        in_specs=[pl.BlockSpec(memory_space=pl.ANY)] * len(arrays),
        out_specs=[pl.BlockSpec(memory_space=pl.ANY)] * len(arrays),
        out_shape=outs,
        scratch_shapes=[
            pltpu.SemaphoreType.DMA((len(shards_of),)),
            pltpu.SemaphoreType.DMA((slots,)),
            pltpu.SemaphoreType.DMA((slots,)),
        ],
        compiler_params=pltpu.CompilerParams(collective_id=0, has_side_effects=True),
        cost_estimate=pl.CostEstimate(flops=0, bytes_accessed=6 * moved, transcendentals=0),
        name="gather_everywhere",
    )(*arrays)


def ring_kernel(cuts, *refs):
    count = len(cuts)
    ins, outs = refs[:count], refs[count : 2 * count]
    slots = [refs[2 * count + 2 * t : 2 * count + 2 * t + 2] for t in range(count)]
    send_sem, recv_sem = refs[4 * count :]
    dp, chip, core = (lax.axis_index(name) for name in ALL)
    chips = lax.axis_size("chip")
    place = place_of(chip, chips)
    ahead, behind = chip_at(place + 1, chips), chip_at(place + chips - 1, chips)
    devices = ((dp, ahead, core), (dp, behind, core))

    barrier = pltpu.get_barrier_semaphore()
    for device in devices:
        pl.semaphore_signal(barrier, inc=1, device_id=device, device_id_type=MESH)
    pl.semaphore_wait(barrier, 2)

    def columns(t, way):
        return pl.ds(0, cuts[t]) if way == 0 else pl.ds(cuts[t], ins[t].shape[-1] - cuts[t])

    def block(t, way, step):
        at = place + 2 * chips - 2 - step if way == 0 else place + 2 + step
        return ins[t].at[chip_at(at, chips), :, columns(t, way)]

    def copy(t, way, step, source):
        return pltpu.make_async_remote_copy(
            src_ref=source,
            dst_ref=slots[t][way].at[step],
            send_sem=send_sem.at[t, way, step],
            recv_sem=recv_sem.at[t, way, step],
            device_id=devices[way],
            device_id_type=MESH,
        )

    pairs = [(t, way) for t in range(count) for way in (0, 1)]
    for t, way in pairs:
        copy(t, way, 0, block(t, way, -1)).start()

    def hop(step, carry):
        for t, way in pairs:
            slot = slots[t][way].at[step - 1]
            copy(t, way, step - 1, slot).wait_recv()
            own = block(t, way, step - 1)[...].astype(jnp.float32)
            slot[...] = (slot[...].astype(jnp.float32) + own).astype(jnp.bfloat16)
            copy(t, way, step, slot).start()
        return carry

    lax.fori_loop(1, chips - 1, hop, 0)
    last = chips - 2
    for t, way in pairs:
        slot = slots[t][way].at[last]
        copy(t, way, last, slot).wait_recv()
        total = slot[...].astype(jnp.float32) + block(t, way, last)[...].astype(jnp.float32)
        outs[t][:, columns(t, way)] = total.astype(outs[t].dtype)

    def finish(step, carry):
        for t, way in pairs:
            copy(t, way, step, slots[t][way].at[step]).wait_send()
        return carry

    lax.fori_loop(0, chips - 1, finish, 0)


def ring_scatter(totals):
    chips = lax.axis_size("chip")
    cuts = [-(-total.shape[2] // (2 * LANES)) * LANES for total in totals]
    vmem = pl.BlockSpec(memory_space=pltpu.VMEM)
    slots = []
    for total, cut in zip(totals, cuts):
        for width in (cut, total.shape[2] - cut):
            slots.append(pltpu.VMEM((chips - 1, total.shape[1], width), jnp.bfloat16))
    return pl.pallas_call(
        functools.partial(ring_kernel, cuts),
        in_specs=[vmem] * len(totals),
        out_specs=[vmem] * len(totals),
        out_shape=[jax.ShapeDtypeStruct(total.shape[1:], jnp.float32) for total in totals],
        scratch_shapes=slots
        + [
            pltpu.SemaphoreType.DMA((len(totals), 2, chips - 1)),
            pltpu.SemaphoreType.DMA((len(totals), 2, chips - 1)),
        ],
        compiler_params=pltpu.CompilerParams(
            collective_id=1, has_side_effects=True, vmem_limit_bytes=VMEM_LIMIT
        ),
        cost_estimate=pl.CostEstimate(
            flops=0, bytes_accessed=sum(8 * total.size for total in totals), transcendentals=0
        ),
        name="ring_scatter",
    )(*totals)


def meet(one, two, bit, send):
    kept, given = jnp.where(bit == 0, one, two), jnp.where(bit == 0, two, one)
    return kept.astype(jnp.float32) + send(given).astype(jnp.float32)


def halve_dp(total):
    columns = total.shape[-1] // 2
    return meet(total[..., :columns], total[..., columns:], lax.axis_index("dp"), swap)


def split_lanes(array):
    half = array.shape[1] // 2
    return jnp.concatenate([pad_lanes(array[:, :half]), pad_lanes(array[:, half:])], axis=1)


def pad_lanes(array):
    columns = array.shape[1]
    return jnp.pad(array, ((0, 0), (0, -columns % LANES)))


def repack_kernel(count, source, target, start, keep, in_ref, out_ref):
    rows = in_ref.shape[0]
    pieces = []
    for block in range(count):
        at = block * source + start
        pieces.append(in_ref[:, at : at + keep].astype(jnp.float32))
        if target > keep:
            pieces.append(jnp.zeros((rows, target - keep), jnp.float32))
    out_ref[...] = jnp.concatenate(pieces, axis=1).astype(out_ref.dtype)


def repack(array, count, source, target, start=0, keep=None):
    keep = min(source, target) if keep is None else keep
    rows = array.shape[0]
    if source == target and keep == source:
        return array
    step = 64 if rows % 64 == 0 else rows
    return pl.pallas_call(
        functools.partial(repack_kernel, count, source, target, start, keep),
        grid=(rows // step,),
        in_specs=[pl.BlockSpec((step, count * source), lambda r: (r, 0))],
        out_specs=pl.BlockSpec((step, count * target), lambda r: (r, 0)),
        out_shape=jax.ShapeDtypeStruct((rows, count * target), array.dtype),
        compiler_params=params(),
        name="repack",
    )(array)


def weave_kernel(count, source, keep, one_ref, two_ref, out_ref):
    pieces = []
    for block in range(count):
        for ref in (one_ref, two_ref):
            pieces.append(ref[:, block * source : block * source + keep].astype(jnp.float32))
    out_ref[...] = jnp.concatenate(pieces, axis=1)


def weave(one, two, count, source, keep):
    rows = one.shape[0]
    return pl.pallas_call(
        functools.partial(weave_kernel, count, source, keep),
        out_shape=jax.ShapeDtypeStruct((rows, 2 * count * keep), jnp.float32),
        compiler_params=pltpu.CompilerParams(vmem_limit_bytes=VMEM_LIMIT),
        name="weave",
    )(one, two)


def convolve(extended, kernel, bias_row):
    length = extended.shape[0] - kernel.shape[1] + 1
    convolved = bias_row
    for offset in range(kernel.shape[1]):
        convolved = convolved + kernel[:, offset] * extended[offset : offset + length, :]
    return convolved


def decay_rates(decay_wide):
    return -jnp.exp(decay_wide.T)


def gating(scanned, gate_path):
    return scanned * silu_gate(gate_path)


def activate(gate_pre, up_pre):
    return silu_gate(gate_pre) * up_pre


def dot(left, right):
    return jnp.dot(left, right, preferred_element_type=jnp.float32)


def dot_rows(left, right):
    return lax.dot_general(left, right, (((0,), (0,)), ((), ())), preferred_element_type=jnp.float32)


def dot_columns(left, right):
    return lax.dot_general(left, right, (((1,), (1,)), ((), ())), preferred_element_type=jnp.float32)


def combine_paths(attended, mamba_path, attention_row, mamba_row):
    return jnp.concatenate(
        [
            rms_norm(attended, attention_row, attended.shape[-1]),
            rms_norm(mamba_path, mamba_row, mamba_path.shape[-1]),
        ],
        axis=-1,
    )


def shards(
    tokens,
    cotangent,
    input_gain,
    merged_weight,
    meta_tokens,
    select_weight,
    step_weight,
    decay_log,
    conv_weight,
    conv_bias,
    step_bias,
    skip_gain,
    attention_gain,
    mamba_gain,
    output_weight,
    second_gain,
    expand_weight,
    down_weight,
):
    parts = lax.axis_size("chip") * lax.axis_size("core")
    position = lax.axis_index(SEQ)
    first = lax.axis_index("dp") == 0
    tokens = tokens[0]
    cotangent = cotangent[0]
    local_len, width = tokens.shape
    query_width = HEADS * HEAD
    key_width = KVHEADS * HEAD
    inner_start = query_width + 2 * key_width
    half = merged_weight.shape[1]
    reach_count = (WINDOW - 1) // local_len + 1
    rows_in = merged_weight.shape[0]
    rows_pad = ceil8(rows_in)
    rows_channel = select_weight.shape[0]
    channel_pad = ceil8(rows_channel)
    rows_joined = output_weight.shape[0]
    joined_pad = ceil8(rows_joined)
    rows_hidden = down_weight.shape[0]
    hidden_half = rows_hidden // 2
    hidden_pad = ceil8(hidden_half)
    hidden_width = parts * hidden_pad
    wide = lambda row: row.astype(jnp.float32)
    conv_bias_wide = wide(conv_bias)
    step_bias_wide = wide(step_bias)
    skip_wide = wide(skip_gain)[None]
    input_row, second_row = wide(input_gain), wide(second_gain)
    attention_row, mamba_row = wide(attention_gain), wide(mamba_gain)

    columns = [weight.shape[1] for weight in (select_weight, step_weight, decay_log, conv_weight)]
    small = jnp.concatenate([select_weight, step_weight, decay_log, conv_weight], axis=1)
    small = jnp.pad(small, ((0, channel_pad - rows_channel), (0, LANES - sum(columns))))
    meta_part = jnp.pad(
        meta_tokens, ((0, rows_pad - rows_in), (0, LANES - meta_tokens.shape[1]))
    )
    small = jnp.concatenate([small, meta_part], axis=0)
    expand_rows = pad_rows(expand_weight, rows_pad)
    expand_halves = [
        repack(expand_rows, parts, rows_hidden, hidden_pad, at, hidden_half)
        for at in (0, hidden_half)
    ]
    down_halves = [
        pad_rows(down_weight[:hidden_half], hidden_pad),
        pad_rows(down_weight[hidden_half:], hidden_pad),
    ]
    cut = output_weight.shape[1]
    merged_full, output_full, small_full, expand_got, down_got, cotangent_got = gather_everywhere(
        [
            pad_lanes(pad_rows(merged_weight, rows_pad)),
            pad_lanes(pad_rows(output_weight, joined_pad)),
            small,
        ],
        (17 * LANES, 4 * LANES, LANES),
        [
            jnp.where(first, expand_halves[1], expand_halves[0]),
            jnp.where(first, down_halves[1], down_halves[0]),
            cotangent,
        ],
    )
    merged_full = merged_full.reshape(2, parts * rows_pad, -1)
    output_full = output_full.reshape(2, parts * joined_pad, -1)
    small_full = small_full.reshape(2, parts, channel_pad + rows_pad, LANES)
    kept = jnp.where(first, expand_halves[0], expand_halves[1])
    expand_mine = jnp.concatenate(
        [jnp.where(first, kept, expand_got), jnp.where(first, expand_got, kept)], axis=1
    )
    kept = jnp.where(first, down_halves[0], down_halves[1])
    down_mine = jnp.concatenate(
        [jnp.where(first, kept, down_got), jnp.where(first, down_got, kept)], axis=1
    )
    small_full, merged_full, expand_mine, down_mine = lax.optimization_barrier(
        (small_full, merged_full, expand_mine, down_mine)
    )
    expand_full = lax.all_gather(expand_mine, SEQ).reshape(parts * rows_pad, 2 * hidden_width)
    down_full = lax.all_gather(down_mine, SEQ).reshape(hidden_width, width)
    cotangent_both = jnp.concatenate([cotangent, cotangent_got], axis=0)
    channel_rows = [part[:, :rows_channel].reshape(MINNER, LANES) for part in small_full]
    pieces, at = [], 0
    for count in columns:
        pieces.append(jnp.concatenate([channel_rows[h][:, at : at + count] for h in (0, 1)], axis=1))
        at += count
    select_full, step_full, decay_full, kernel_full = pieces
    meta_full = jnp.concatenate(
        [
            small_full[h][:, channel_pad:, : meta_tokens.shape[1]].reshape(
                parts * rows_pad, meta_tokens.shape[1]
            )
            for h in (0, 1)
        ],
        axis=1,
    )

    tokens_wide = wide(tokens)
    normed_wide, norm_back = jax.vjp(lambda v, g: rms_norm(v, g, width), tokens_wide, input_row)
    normed = repack(normed_wide.astype(jnp.bfloat16), parts, rows_in, rows_pad)
    input_row_pad = jnp.pad(
        input_row.reshape(parts, rows_in), ((0, 0), (0, rows_pad - rows_in))
    ).reshape(parts * rows_pad)
    meta_wide, meta_back = jax.vjp(
        lambda v, g: rms_norm(v, g, width), wide(meta_full).T, input_row_pad
    )
    stacked_normed = jnp.concatenate([normed, meta_wide.astype(jnp.bfloat16)], axis=0)
    projected_one = dot(stacked_normed, merged_full[0])
    projected_two = dot(normed, merged_full[1])
    queries = projected_one[:local_len, :query_width].astype(jnp.bfloat16)
    pairs_own = projected_one[:local_len, query_width:inner_start].astype(jnp.bfloat16)
    meta_pairs = projected_one[local_len:, query_width:inner_start].astype(jnp.bfloat16)
    inner_path = jnp.concatenate(
        [
            projected_one[:local_len, inner_start:half].astype(jnp.bfloat16),
            projected_two[:, : inner_start + MINNER - half].astype(jnp.bfloat16),
        ],
        axis=1,
    )
    gate_path = projected_two[:, inner_start + MINNER - half : half]

    pairs = jnp.concatenate(
        [meta_pairs]
        + [from_behind(pairs_own, behind) for behind in range(reach_count, 0, -1)]
        + [pairs_own],
        axis=0,
    )
    where = jnp.reshape(position, (1,)).astype(jnp.int32)
    heads_first = lambda rows: jnp.moveaxis(rows.reshape(rows.shape[0], KVHEADS, HEAD), 1, 0)
    keys, values = heads_first(pairs[:, :key_width]), heads_first(pairs[:, key_width:])
    key_turned, value_turned = pairs[:, :key_width].T, pairs[:, key_width:].T
    query_turned = queries.T
    attended_turned, logs = attend(where, query_turned, keys, value_turned, reach_count + 1)
    attended = attended_turned.T

    previous = from_behind(inner_path[local_len - (CONV - 1) :], 1)
    extended = wide(jnp.concatenate([previous, inner_path], axis=0))
    kernel = wide(kernel_full)
    convolved, convolve_back = jax.vjp(convolve, extended, kernel, conv_bias_wide)
    activated, silu_back = jax.vjp(silu_gate, convolved)
    signal = activated.astype(jnp.bfloat16)
    selected = dot(signal, select_full)
    step_raw = selected[:, :DTR].astype(jnp.bfloat16)
    spread_lanes = lambda mix: jnp.broadcast_to(mix[:, :, None], (local_len, STATE, LANES))
    write_wide = spread_lanes(selected[:, DTR : DTR + STATE])
    read_wide = spread_lanes(selected[:, DTR + STATE :])
    step_pre = dot_columns(step_raw, step_full) + step_bias_wide
    step_size = softplus(step_pre)
    decays, decay_back = jax.vjp(decay_rates, wide(decay_full))
    ends = scan_ends(step_size, signal, write_wide, decays)
    ends, expand_full = lax.optimization_barrier((ends, expand_full))
    total = jnp.sum(step_size, axis=0, keepdims=True)
    coarse = lax.reduce_precision(total, 8, 7)
    carried = lax.all_gather(
        jnp.concatenate([ends, coarse, total - coarse], axis=0).astype(jnp.bfloat16), SEQ
    )
    totals = wide(carried[:, STATE : STATE + 1]) + wide(carried[:, STATE + 1 :])
    scanned, enter = scan_forward(
        where, step_size, signal, write_wide, read_wide, decays, skip_wide, totals, carried[:, :STATE]
    )
    mamba_path, gating_back = jax.vjp(gating, scanned, gate_path)
    joined_wide, paths_back = jax.vjp(
        combine_paths, attended, mamba_path, attention_row, mamba_row
    )
    joined = repack(joined_wide.astype(jnp.bfloat16), parts, rows_joined, joined_pad)
    hidden = tokens_wide + 0.5 * jnp.concatenate(
        [dot(joined, output_full[0])[:, :cut], dot(joined, output_full[1])[:, :cut]], axis=1
    )

    normed_two_wide, norm_two_back = jax.vjp(lambda v, g: rms_norm(v, g, width), hidden, second_row)
    normed_two = repack(normed_two_wide.astype(jnp.bfloat16), parts, rows_in, rows_pad)
    normed_both = jnp.concatenate([normed_two, swap(normed_two)], axis=0)
    expanded = dot(normed_both, expand_full)
    active_wide, activate_back = jax.vjp(
        activate, expanded[:, :hidden_width], expanded[:, hidden_width:]
    )
    active = active_wide.astype(jnp.bfloat16)
    down_out = dot(active, down_full)
    block_output = (
        hidden + down_out[:local_len] + wide(swap(down_out[local_len:].astype(jnp.bfloat16)))
    ).astype(jnp.bfloat16)

    hidden_columns = parity_columns(active, parts, hidden_pad)
    down_grad = grad_parts(hidden_columns, pad_lanes(cotangent_both))
    down_sum = scatter_rows(down_grad, hidden_pad)
    active_grad = dot_columns(cotangent_both, down_full)
    gate_grad, up_grad = activate_back(active_grad)
    expand_in = jnp.concatenate(
        [gate_grad.astype(jnp.bfloat16), up_grad.astype(jnp.bfloat16)], axis=1
    )
    second_both = dot_columns(expand_in, expand_full)
    second_both, block_output = lax.optimization_barrier((second_both, block_output))
    second_normed_grad = repack(
        second_both[:local_len] + wide(swap(second_both[local_len:].astype(jnp.bfloat16))),
        parts,
        rows_pad,
        rows_in,
    )
    hidden_part, second_gain_grad = norm_two_back(second_normed_grad)
    hidden_grad = hidden_part + wide(cotangent)
    mixed_in = hidden_grad.astype(jnp.bfloat16)
    mixed_split = split_lanes(mixed_in)
    cut_pad = mixed_split.shape[1] // 2
    joined_grad = repack(
        0.5
        * (
            dot_columns(mixed_split[:, :cut_pad], output_full[0])
            + dot_columns(mixed_split[:, cut_pad:], output_full[1])
        ),
        parts,
        joined_pad,
        rows_joined,
    )
    attended_grad, mamba_grad, attention_gain_grad, mamba_gain_grad = paths_back(joined_grad)
    scanned_grad, gate_path_grad = gating_back(mamba_grad)
    own_pull = scan_pulls(step_size, scanned_grad, read_wide, decays).astype(jnp.bfloat16)
    pulls = lax.all_gather(own_pull, SEQ)

    normed_both, joined, own_pull, down_sum = lax.optimization_barrier(
        (normed_both, joined, own_pull, down_sum)
    )
    both_split = parity_columns(normed_both, parts, rows_pad)
    gate_total = grad_parts(both_split, expand_in[:, :hidden_width])
    up_total = grad_parts(both_split, expand_in[:, hidden_width:])
    output_grad = grad_parts(parity_columns(joined, parts, joined_pad), mixed_split, 0.5)
    kept = jnp.where(first, down_sum[:, :cut], down_sum[:, cut : 2 * cut])
    got = swap(jnp.where(first, down_sum[:, cut : 2 * cut], down_sum[:, :cut]))
    down_out_grad = jnp.concatenate(
        [
            jnp.where(first, kept, got)[:hidden_half],
            jnp.where(first, got, kept)[:hidden_half],
        ],
        axis=0,
    )
    attended_in, gate_total, up_total, output_grad, pulls, down_out_grad = lax.optimization_barrier(
        (attended_grad.astype(jnp.bfloat16), gate_total, up_total, output_grad, pulls, down_out_grad)
    )
    gate_sum = scatter_rows(gate_total, rows_pad)
    up_sum = scatter_rows(up_total, rows_pad)
    output_grad = halve_dp(output_grad).astype(jnp.bfloat16)

    query_grad_turned, key_grads, value_grads = attend_back(
        where,
        query_turned,
        attended_in.T,
        attended_turned,
        logs,
        keys,
        values,
        key_turned,
        reach_count + 1,
    )
    heads_last = lambda grads: jnp.moveaxis(grads, 0, 1).reshape(grads.shape[1], key_width)
    pair_grads = jnp.concatenate([heads_last(key_grads), heads_last(value_grads)], axis=1)
    meta_pair_grad, window_grad = pair_grads[:META], pair_grads[META:]
    own_grad = window_grad[reach_count * local_len :]
    for behind in range(1, reach_count + 1):
        own_grad = own_grad + wide(
            from_behind(
                window_grad[
                    (reach_count - behind) * local_len : (reach_count - behind + 1) * local_len
                ].astype(jnp.bfloat16),
                -behind,
            )
        )

    own_grad, meta_pair_grad, gate_sum, output_grad = lax.optimization_barrier(
        (own_grad, meta_pair_grad, gate_sum, output_grad)
    )
    with_meta = lambda rows, meta: jnp.concatenate([rows, meta], axis=0)
    query_in = with_meta(query_grad_turned.T, jnp.zeros((META, query_width), jnp.bfloat16))
    pair_in = with_meta(own_grad, meta_pair_grad).astype(jnp.bfloat16)
    gate_in = with_meta(gate_path_grad.astype(jnp.bfloat16), jnp.zeros((META, MINNER), jnp.bfloat16))
    normed_split = parity_columns(stacked_normed, parts, rows_pad)
    early_grad = grad_parts(
        normed_split, pad_lanes(jnp.concatenate([gate_in, query_in, pair_in], axis=1))
    )
    scanned_grad, early_grad = lax.optimization_barrier((scanned_grad, early_grad))
    early_sum = scatter_rows(early_grad, rows_pad)
    signal_grad, step_grad, write_parts, read_parts, decays_grad, skip_parts = scan_backward(
        where,
        step_size,
        signal,
        scanned_grad,
        write_wide,
        read_wide,
        decays,
        skip_wide,
        enter,
        totals,
        pulls,
    )
    step_grad, up_sum = lax.optimization_barrier((step_grad, up_sum))
    step_pre_grad = step_grad * jax.nn.sigmoid(step_pre)
    step_in = step_pre_grad.astype(jnp.bfloat16)
    step_weight_grad = dot_rows(step_in, step_raw)
    selected_in = jnp.concatenate(
        [dot(step_in, step_full), jnp.sum(write_parts, axis=-1), jnp.sum(read_parts, axis=-1)],
        axis=-1,
    ).astype(jnp.bfloat16)
    select_grad = dot_rows(signal, selected_in)
    signal_grad = signal_grad + dot_columns(selected_in, select_full)
    extended_grad, kernel_grad, conv_bias_grad = convolve_back(silu_back(signal_grad)[0])
    returned_tail = wide(from_behind(extended_grad[: CONV - 1].astype(jnp.bfloat16), -1))
    inner_grad = extended_grad[CONV - 1 :] + jnp.pad(
        returned_tail, ((local_len - (CONV - 1), 0), (0, 0))
    )
    decay_grad = decay_back(decays_grad)[0]

    inner_in = with_meta(inner_grad.astype(jnp.bfloat16), jnp.zeros((META, MINNER), jnp.bfloat16))
    inner_cut = half - inner_start
    inner_first = -(-inner_cut // LANES) * LANES
    inner_grads = grad_parts(
        normed_split,
        jnp.concatenate([pad_lanes(inner_in[:, :inner_cut]), pad_lanes(inner_in[:, inner_cut:])], axis=1),
    )
    one_in = pad_lanes(jnp.concatenate([query_in, pair_in, inner_in[:, :inner_cut]], axis=1))
    two_in = pad_lanes(
        jnp.concatenate([inner_in[:local_len, inner_cut:], gate_in[:local_len]], axis=1)
    )
    stacked_grad = dot_columns(one_in, merged_full[0])
    normed_grad = repack(
        stacked_grad[:local_len] + dot_columns(two_in, merged_full[1]), parts, rows_pad, rows_in
    )
    meta_rows_grad, meta_gain_grad = meta_back(stacked_grad[local_len:])
    tokens_part, input_gain_part = norm_back(normed_grad)
    tokens_grad = hidden_grad + tokens_part
    input_gain_grad = input_gain_part + (
        meta_gain_grad.reshape(parts, rows_pad)[:, :rows_in].reshape(width)
    )

    count = meta_tokens.shape[1]
    meta_grads = jnp.pad(
        meta_rows_grad.T.reshape(parts, rows_pad, META),
        ((0, 0), (0, channel_pad - rows_pad), (0, 0)),
    )
    sides = []
    for h in (0, 1):
        cuts = [
            grad[:, h * size : (h + 1) * size]
            for grad, size in zip((select_grad, step_weight_grad, decay_grad, kernel_grad), columns)
        ]
        side = jnp.concatenate(cuts, axis=1).reshape(parts, rows_channel, sum(columns))
        side = jnp.pad(
            side, ((0, 0), (0, channel_pad - rows_channel), (0, LANES - sum(columns)))
        )
        meta_side = meta_grads[:, :, h * count : (h + 1) * count]
        sides += [side, jnp.pad(meta_side, ((0, 0), (0, 0), (0, LANES - count)))]
    small_grads = jnp.concatenate(sides, axis=2).astype(jnp.bfloat16)
    small_grads = small_grads.reshape(parts // 2, 2, channel_pad, 4 * LANES)
    small_sum = meet(
        small_grads[:, 0],
        small_grads[:, 1],
        lax.axis_index("core"),
        lambda array: swap(array, "core"),
    )
    inner_grads, early_sum = lax.optimization_barrier((inner_grads, early_sum))
    inner_sum, output_out, small_sum = ring_scatter(
        [
            inner_grads.reshape(parts // 2, rows_pad, -1),
            output_grad.reshape(parts // 2, joined_pad, -1),
            small_sum.astype(jnp.bfloat16),
        ]
    )
    output_out = output_out[:rows_joined, :cut]
    pair_early = jnp.pad(
        early_sum[:, MINNER : MINNER + inner_start], ((0, 0), (0, MINNER - inner_start))
    )
    early_out = meet(
        pair_early,
        early_sum[:, :MINNER],
        lax.axis_index("dp"),
        lambda array: swap(array.astype(jnp.bfloat16)),
    )[:rows_in]
    small_sum = halve_dp(small_sum)
    inner_one, inner_two = inner_sum[:, :inner_first], inner_sum[:, inner_first:]
    inner_two = jnp.pad(inner_two, ((0, 0), (0, inner_first - inner_two.shape[1])))
    inner_out = meet(
        inner_one, inner_two, lax.axis_index("dp"), lambda array: swap(array.astype(jnp.bfloat16))
    )[:rows_in]
    small_outs, at = [], 0
    for size in columns:
        small_outs.append(small_sum[:rows_channel, at : at + size])
        at += size
    meta_sum = small_sum[:rows_in, LANES : LANES + count]

    vectors = (
        second_gain_grad,
        attention_gain_grad,
        mamba_gain_grad,
        jnp.sum(skip_parts, axis=0),
        jnp.sum(step_pre_grad, axis=0),
        conv_bias_grad,
        input_gain_grad,
    )
    flat = jnp.concatenate(vectors)
    padded = -(-flat.shape[0] // (8 * LANES)) * 8 * LANES
    flat = sum_everywhere(jnp.pad(flat, (0, padded - flat.shape[0])).reshape(-1, LANES))
    flat = flat.reshape(-1)
    sums, at = [], 0
    for vector in vectors:
        sums.append(flat[at : at + vector.shape[0]])
        at += vector.shape[0]

    rest = half - MINNER
    merged_out = jnp.where(
        first,
        jnp.concatenate([early_out[:, :inner_start], inner_out[:, :inner_cut]], axis=1),
        jnp.concatenate([inner_out[:, :rest], early_out], axis=1),
    )
    gate_part, up_part = gate_sum, up_sum
    kept = jnp.where(first, gate_part, up_part)
    got = swap(jnp.where(first, up_part, gate_part))
    expand_out = weave(
        jnp.where(first, kept, got), jnp.where(first, got, kept), parts, hidden_pad, hidden_half
    )[:rows_in]
    return (
        block_output[None],
        tokens_grad[None],
        sums[6],
        merged_out,
        meta_sum,
        small_outs[0],
        small_outs[1],
        small_outs[2],
        small_outs[3],
        sums[5],
        sums[4],
        sums[3],
        sums[1],
        sums[2],
        output_out,
        sums[0],
        expand_out,
        wide(down_out_grad),
    )


def solution(mesh):
    split = Mesh(mesh.devices.reshape(2, -1, 2), ALL)
    rows, matrix, copied = P("dp", SEQ, None), P(SEQ, "dp"), P()
    return jax.shard_map(
        shards,
        mesh=split,
        in_specs=(rows, rows, copied) + (matrix,) * 6 + (copied,) * 5 + (matrix, copied, matrix, matrix),
        out_specs=(rows, rows, copied) + (matrix,) * 6 + (copied,) * 5 + (matrix, copied, matrix, matrix),
        check_vma=False,
    )
```
